512 devices in a mesh: ix: 4 (over x), iy: 8 (over y, core), depth: 16 (over z).
Axes of the slice: x: 4, y: 4, z: 16, core: 2. Of those that a mesh axis runs over, the one named last changes fastest.
Arguments:
- density: float32 [1024, 1024, 512], P('depth', 'iy', 'ix'), may hold values from -4 to 4
- color_coeffs: float32 [3, 4], replicated, may hold values from -1 to 1
- opacity_coeffs: float32 [4], replicated, may hold values from -1 to 1
- light: float32 [3], replicated, may hold values from -1 to 1
Outputs:
- image: float32 [4, 1024, 512], P(None, ('iy', 'depth'), 'ix')
The draws below stay inside these ranges and needn't reach their ends.
All inputs are finite; a program needn't handle non-finite values.
Results may differ from the reference program's by a relative error of at most 0.0003.
Values sent between devices are 32-bit elements; how exact they have to be, the bound alone decides.
A program may use at most 64 MiB of HBM per device.

```python
import jax
import jax.numpy as jnp
from jax import lax

BY = 128
POLY = 4
NX = 512
NY = 1024
NZ = 1024


def levels(stream_key, dims, pieces, low, high):
    loudness, own = 1.0, jax.random.fold_in(stream_key, 6)
    for dim, parts in pieces:
        steps = jnp.exp(jax.random.uniform(jax.random.fold_in(own, dim), (parts,), jnp.float32, low / len(pieces), high / len(pieces)))
        loudness = loudness * jnp.repeat(steps, dims[dim] // parts).reshape([-1 if axis == dim else 1 for axis in range(len(dims))])
    return loudness


def normal_values(stream_key, shape, width, most, split=(), held_as=jnp.bfloat16):
    values = width * jax.random.normal(stream_key, shape, jnp.float32)
    if split:
        values = values * levels(stream_key, shape, split, -0.22, 0.18)
    return jnp.clip(values, -most, most).astype(held_as)


def setup_inputs(seed: int = 0) -> dict:
    splits = jax.random.split(jax.random.key(seed), 5)
    return {
        "density": normal_values(splits[0], (NZ, NY, NX), 1.0, 4.0, ((0, 16), (1, 8), (2, 4)), jnp.float32),
        "color_coeffs": jnp.clip(jax.random.uniform(splits[1], (3, POLY), jnp.float32, -1.0, 1.0), -1.0, 1.0),
        "opacity_coeffs": jnp.clip(jax.random.uniform(splits[2], (POLY,), jnp.float32, -1.0, 1.0), -1.0, 1.0),
        "light": jnp.clip(jax.random.uniform(splits[3], (3,), jnp.float32, -1.0, 1.0), -1.0, 1.0),
    }


def polynomial(coeffs, values):
    result = jnp.zeros_like(values) + coeffs[-1]
    for degree in range(coeffs.shape[0] - 2, -1, -1):
        result = result * values + coeffs[degree]
    return result

def shade_block(padded, color_coeffs, opacity_coeffs, light, depth_total):
    centre = padded[1:-1, 1:-1, 1:-1]
    grad_z = 0.5 * (padded[2:, 1:-1, 1:-1] - padded[:-2, 1:-1, 1:-1])
    grad_y = 0.5 * (padded[1:-1, 2:, 1:-1] - padded[1:-1, :-2, 1:-1])
    grad_x = 0.5 * (padded[1:-1, 1:-1, 2:] - padded[1:-1, 1:-1, :-2])
    scaled = centre * 0.25
    extinction = 3.0 / depth_total * polynomial(opacity_coeffs, scaled) ** 2
    facing = grad_x * light[0] + grad_y * light[1] + grad_z * light[2]
    shading = 0.3 + 0.7 * jnp.abs(facing) / jnp.sqrt(grad_x * grad_x + grad_y * grad_y + grad_z * grad_z + 1.0)
    before = jnp.cumsum(extinction, 0) - extinction
    weight = jnp.exp(-before) * (1.0 - jnp.exp(-extinction)) * shading
    colors = [lax.optimization_barrier(jnp.sum(weight * polynomial(color_coeffs[channel], scaled) ** 2, 0)) for channel in range(3)]
    optical = lax.optimization_barrier(jnp.sum(extinction, 0))
    return jnp.stack(colors + [optical])

def reference(density, color_coeffs, opacity_coeffs, light):
    padded = jnp.pad(density, 1)
    slabs = NY // BY

    def one_slab(number):
        start = (number * BY).astype(jnp.int32)
        zero = jnp.zeros((), jnp.int32)
        block = lax.dynamic_slice(padded, (zero, start, zero), (NZ + 2, BY + 2, NX + 2))
        partial_value = shade_block(block, color_coeffs, opacity_coeffs, light, float(NZ))
        return jnp.concatenate([partial_value[:3], jnp.exp(-partial_value[3:])], 0)
    result = lax.map(one_slab, jnp.arange(slabs, dtype=jnp.int32))
    return jnp.transpose(result, (1, 0, 2, 3)).reshape(4, NY, NX)
```

```python
import functools
import math

import jax
import jax.numpy as jnp
from jax import lax
from jax.experimental import pallas as pl
from jax.experimental.pallas import tpu as pltpu
from jax.sharding import PartitionSpec as P

MESH = pl.DeviceIdType.MESH
LANES = 128
ROWS = 8
CHUNKS = 4
UNROLL = 8


def kernel(
    layers,
    density,
    color,
    opacity,
    light,
    image,
    brick,
    x_out,
    x_in,
    y_out,
    y_in,
    x_halo,
    sent,
    parts,
    color_s,
    opacity_s,
    light_s,
    load_sem,
    coeff_sem,
    halo_send,
    halo_recv,
    part_send,
    part_recv,
):
    brick_z, brick_y, _ = density.shape
    blocks = brick_y // ROWS
    ix, nx = lax.axis_index("ix"), lax.axis_size("ix")
    iy, ny = lax.axis_index("iy"), lax.axis_size("iy")
    me = lax.axis_index("depth")

    barrier = pltpu.get_barrier_semaphore()
    sides = (("ix", ix, nx), ("iy", iy, ny))

    def greet(step, carry):
        pl.semaphore_signal(
            barrier, inc=1, device_id={"depth": lax.rem(me + step, layers)}, device_id_type=MESH
        )
        return carry

    lax.fori_loop(1, layers, greet, 0)
    for axis, place, size in sides:

        @pl.when(place > 0)
        def _():
            pl.semaphore_signal(barrier, inc=1, device_id={axis: place - 1}, device_id_type=MESH)

        @pl.when(place < size - 1)
        def _():
            pl.semaphore_signal(barrier, inc=1, device_id={axis: place + 1}, device_id_type=MESH)

    span = brick_y // CHUNKS

    def load(chunk):
        return pltpu.make_async_copy(
            density.at[:, pl.ds(chunk * span, span), :],
            brick.at[pl.ds(1, brick_z), pl.ds(ROWS + chunk * span, span), :],
            load_sem.at[chunk],
        )

    for chunk in range(CHUNKS):
        load(chunk).start()
    coeffs = [
        pltpu.make_async_copy(source, target, coeff_sem.at[number])
        for number, (source, target) in enumerate(
            ((color, color_s), (opacity, opacity_s), (light, light_s))
        )
    ]
    for copy in coeffs:
        copy.start()

    lane = lax.broadcasted_iota(jnp.int32, (ROWS, LANES), 1)
    even = lax.rem(lane, 2) == 0
    pair = lane // 2
    per_chunk = blocks // CHUNKS

    def pack(chunk, carry):
        load(chunk).wait()
        base = pl.multiple_of(ROWS + chunk * span, ROWS)
        packed = [jnp.zeros((ROWS, LANES), jnp.float32) for _ in range(per_chunk)]
        for z in range(brick_z):
            here = pair == z
            for k in range(per_chunk):
                v = brick[z + 1, pl.ds(base + ROWS * k, ROWS), :]
                packed[k] = jnp.where(here, pltpu.roll(v, 2 * z + 1, 1), packed[k])
        half = pl.multiple_of(chunk * (span // 2), ROWS)
        for k in range(0, per_chunk, 2):
            a, b = packed[k], packed[k + 1]
            at = pl.ds(half + ROWS * (k // 2), ROWS)
            x_out[0, at, :] = jnp.where(even, pltpu.roll(a, LANES - 1, 1), b)
            x_out[1, at, :] = jnp.where(even, a, pltpu.roll(b, 1, 1))
        return carry

    lax.fori_loop(0, CHUNKS, pack, 0)
    y_out[0] = brick[pl.ds(1, brick_z), ROWS, :]
    y_out[1] = brick[pl.ds(1, brick_z), ROWS + brick_y - 1, :]

    greeted = layers - 1
    for _, place, size in sides:
        greeted = greeted + jnp.where(place > 0, 1, 0) + jnp.where(place < size - 1, 1, 0)
    pl.semaphore_wait(barrier, greeted)

    data = pl.ds(ROWS, brick_y)
    halos = []
    for number, (axis, place, size, down, up) in enumerate(
        (
            ("ix", ix, nx, (x_out.at[0], x_in.at[1]), (x_out.at[1], x_in.at[0])),
            ("iy", iy, ny, (y_out.at[0], y_in.at[1]), (y_out.at[1], y_in.at[0])),
            (
                "depth",
                me,
                layers,
                (density.at[0], brick.at[brick_z + 1, data, :]),
                (density.at[brick_z - 1], brick.at[0, data, :]),
            ),
        )
    ):
        lower, upper = place > 0, place < size - 1
        for way, (go, come, (source, target), step) in enumerate(
            ((lower, upper, down, -1), (upper, lower, up, 1))
        ):
            copy = pltpu.make_async_remote_copy(
                src_ref=source,
                dst_ref=target,
                send_sem=halo_send.at[2 * number + way],
                recv_sem=halo_recv.at[2 * number + way],
                device_id={axis: place + step},
                device_id_type=MESH,
            )
            halos.append((copy, go, come, target))
    for copy, go, come, target in halos:

        @pl.when(go)
        def _():
            copy.start()

        @pl.when(jnp.logical_not(come))
        def _():
            target[...] = jnp.zeros(target.shape, jnp.float32)

    for copy in coeffs:
        copy.wait()
    root = math.sqrt(3.0 / (brick_z * layers) * math.log2(math.e))
    o0, o1, o2, o3 = (opacity_s[k] * (root / 4.0**k) for k in range(4))
    lx, ly, lz = (0.7 * light_s[k] for k in range(3))
    squares = []
    for channel in range(3):
        c0, c1, c2, c3 = (color_s[channel, k] for k in range(4))
        squares.append(
            [
                c0 * c0,
                2.0 * c0 * c1 / 4.0,
                (2.0 * c0 * c2 + c1 * c1) / 16.0,
                2.0 * (c0 * c3 + c1 * c2) / 64.0,
                (2.0 * c1 * c3 + c2 * c2) / 256.0,
                2.0 * c2 * c3 / 1024.0,
                c3 * c3 / 4096.0,
            ]
        )

    for copy, go, come, target in halos:

        @pl.when(come)
        def _():
            copy.wait_recv()

    def unpack(k, carry):
        at = pl.ds(pl.multiple_of(ROWS * k, ROWS), ROWS)
        left, right = x_in[0, at, :], x_in[1, at, :]
        first = pl.multiple_of(2 * ROWS * k, ROWS)
        x_halo[pl.ds(first, ROWS), :] = jnp.where(even, left, pltpu.roll(right, 1, 1))
        x_halo[pl.ds(first + ROWS, ROWS), :] = jnp.where(
            even, pltpu.roll(left, LANES - 1, 1), right
        )
        return carry

    lax.fori_loop(0, blocks // 2, unpack, 0)
    brick[pl.ds(1, brick_z), ROWS - 1, :] = y_in[0]
    brick[pl.ds(1, brick_z), ROWS + brick_y, :] = y_in[1]

    is_first, is_last = lane == 0, lane == LANES - 1

    def part_copy(block):
        return pltpu.make_async_remote_copy(
            src_ref=sent.at[block],
            dst_ref=parts.at[me],
            send_sem=part_send.at[block],
            recv_sem=part_recv.at[me],
            device_id={"depth": block},
            device_id_type=MESH,
        )

    def cast(block):
        row = pl.multiple_of(ROWS * block, ROWS)
        halo = x_halo[pl.ds(row, ROWS), :]

        def cells(group, carry):
            total, before, moments = carry
            moments = list(moments)
            turned = pltpu.roll(halo, lax.rem(LANES - 2 * UNROLL * group, LANES), 1)
            for k in range(UNROLL):
                z = group * UNROLL + k
                v = brick[z + 1, pl.ds(row + ROWS, ROWS), :]
                edge = pltpu.roll(turned, LANES - (2 * k + 1), 1)
                gx = pltpu.roll(jnp.where(is_first, edge, v), LANES - 1, 1) - pltpu.roll(
                    jnp.where(is_last, edge, v), 1, 1
                )
                gy = (
                    brick[z + 1, pl.ds(row + ROWS + 1, ROWS), :]
                    - brick[z + 1, pl.ds(row + ROWS - 1, ROWS), :]
                )
                gz = (
                    brick[z + 2, pl.ds(row + ROWS, ROWS), :]
                    - brick[z, pl.ds(row + ROWS, ROWS), :]
                )
                facing = gx * lx + gy * ly + gz * lz
                norm = (gx * gx + gy * gy) + (gz * gz + 4.0)
                shading = jnp.abs(facing) * lax.rsqrt(norm) + 0.3
                p = ((o3 * v + o2) * v + o1) * v + o0
                total = total - p * p
                after = jnp.exp2(total)
                weight = (before - after) * shading
                before = after
                moments[0] = moments[0] + weight
                for degree in range(1, 7):
                    weight = weight * v
                    moments[degree] = moments[degree] + weight
            return total, before, tuple(moments)

        zero = jnp.zeros((ROWS, LANES), jnp.float32)
        _, clear, moments = lax.fori_loop(
            0, brick_z // UNROLL, cells, (zero, zero + 1.0, (zero,) * 7)
        )
        for channel in range(3):
            q = squares[channel]
            value = q[0] * moments[0]
            for degree in range(1, 7):
                value = value + q[degree] * moments[degree]
            sent[block, channel] = value
        sent[block, 3] = clear

    def others(step, carry):
        half = (step + 1) // 2
        hop = jnp.where(lax.rem(step, 2) == 0, layers // 2 + half, layers // 2 - half)
        block = lax.rem(me + hop, layers)
        cast(block)
        part_copy(block).start()
        return carry

    lax.fori_loop(0, layers - 1, others, 0)
    cast(me)

    def composite(layer, carry):
        red, green, blue, clear = carry

        @pl.when(layer != me)
        def _():
            pltpu.make_async_remote_copy(
                src_ref=sent.at[layer],
                dst_ref=parts.at[layer],
                send_sem=part_send.at[layer],
                recv_sem=part_recv.at[layer],
                device_id={"depth": layer},
                device_id_type=MESH,
            ).wait_recv()

        @pl.when(layer == me)
        def _():
            parts[layer] = sent[layer]

        return (
            red + clear * parts[layer, 0],
            green + clear * parts[layer, 1],
            blue + clear * parts[layer, 2],
            clear * parts[layer, 3],
        )

    zero = jnp.zeros((ROWS, LANES), jnp.float32)
    result = lax.fori_loop(0, layers, composite, (zero, zero, zero, zero + 1.0))
    for channel in range(4):
        image[channel] = result[channel]

    def finish(step, carry):
        part_copy(lax.rem(me + step, layers)).wait_send()
        return carry

    lax.fori_loop(1, layers, finish, 0)
    for copy, go, come, target in halos:

        @pl.when(go)
        def _():
            copy.wait_send()


def per_device(density, color_coeffs, opacity_coeffs, light):
    layers = lax.axis_size("depth")
    brick_z, brick_y, brick_x = density.shape
    blocks = brick_y // ROWS
    f32 = jnp.float32
    return pl.pallas_call(
        functools.partial(kernel, layers),
        out_shape=jax.ShapeDtypeStruct((4, ROWS, brick_x), f32),
        in_specs=[pl.BlockSpec(memory_space=pl.ANY)] * 4,
        out_specs=pl.BlockSpec(memory_space=pltpu.VMEM),
        scratch_shapes=[
            pltpu.VMEM((brick_z + 2, brick_y + 2 * ROWS, brick_x), f32),
            pltpu.VMEM((2, brick_y // 2, LANES), f32),
            pltpu.VMEM((2, brick_y // 2, LANES), f32),
            pltpu.VMEM((2, brick_z, LANES), f32),
            pltpu.VMEM((2, brick_z, LANES), f32),
            pltpu.VMEM((brick_y, LANES), f32),
            pltpu.VMEM((blocks, 4, ROWS, LANES), f32),
            pltpu.VMEM((layers, 4, ROWS, LANES), f32),
            pltpu.SMEM((3, 4), f32),
            pltpu.SMEM((4,), f32),
            pltpu.SMEM((3,), f32),
            pltpu.SemaphoreType.DMA((CHUNKS,)),
            pltpu.SemaphoreType.DMA((3,)),
            pltpu.SemaphoreType.DMA((6,)),
            pltpu.SemaphoreType.DMA((6,)),
            pltpu.SemaphoreType.DMA((blocks,)),
            pltpu.SemaphoreType.DMA((layers,)),
        ],
        compiler_params=pltpu.CompilerParams(
            collective_id=0, has_side_effects=True, vmem_limit_bytes=24 << 20
        ),
    )(density, color_coeffs, opacity_coeffs, light)


def solution(mesh):
    return jax.shard_map(
        per_device,
        mesh=mesh,
        in_specs=(P("depth", "iy", "ix"), P(), P(), P()),
        out_specs=P(None, ("iy", "depth"), "ix"),
        check_vma=False,
    )
```

```python
import functools
import math

import jax
import jax.numpy as jnp
from jax import lax
from jax.experimental import pallas as pl
from jax.experimental.pallas import tpu as pltpu
from jax.sharding import PartitionSpec as P

MESH = pl.DeviceIdType.MESH
LANES = 128
ROWS = 8
CHUNKS = 4


def kernel(
    layers,
    density,
    color,
    opacity,
    light,
    image,
    brick,
    x_out,
    x_in,
    y_out,
    y_in,
    x_halo,
    sent,
    parts,
    color_s,
    opacity_s,
    light_s,
    load_sem,
    coeff_sem,
    halo_send,
    halo_recv,
    part_send,
    part_recv,
):
    brick_z, brick_y, _ = density.shape
    blocks = brick_y // ROWS
    ix, nx = lax.axis_index("ix"), lax.axis_size("ix")
    iy, ny = lax.axis_index("iy"), lax.axis_size("iy")
    me = lax.axis_index("depth")

    barrier = pltpu.get_barrier_semaphore()
    sides = (("ix", ix, nx), ("iy", iy, ny))

    def greet(step, carry):
        pl.semaphore_signal(
            barrier, inc=1, device_id={"depth": lax.rem(me + step, layers)}, device_id_type=MESH
        )
        return carry

    lax.fori_loop(1, layers, greet, 0)
    for axis, place, size in sides:

        @pl.when(place > 0)
        def _():
            pl.semaphore_signal(barrier, inc=1, device_id={axis: place - 1}, device_id_type=MESH)

        @pl.when(place < size - 1)
        def _():
            pl.semaphore_signal(barrier, inc=1, device_id={axis: place + 1}, device_id_type=MESH)

    span = brick_y // CHUNKS

    def load(chunk):
        return pltpu.make_async_copy(
            density.at[:, pl.ds(chunk * span, span), :],
            brick.at[pl.ds(1, brick_z), pl.ds(ROWS + chunk * span, span), :],
            load_sem.at[chunk],
        )

    for chunk in range(CHUNKS):
        load(chunk).start()
    coeffs = [
        pltpu.make_async_copy(source, target, coeff_sem.at[number])
        for number, (source, target) in enumerate(
            ((color, color_s), (opacity, opacity_s), (light, light_s))
        )
    ]
    for copy in coeffs:
        copy.start()

    lane = lax.broadcasted_iota(jnp.int32, (ROWS, LANES), 1)
    even = lax.rem(lane, 2) == 0
    pair = lane // 2
    per_chunk = blocks // CHUNKS

    def pack(chunk, carry):
        load(chunk).wait()
        base = pl.multiple_of(ROWS + chunk * span, ROWS)
        packed = [jnp.zeros((ROWS, LANES), jnp.float32) for _ in range(per_chunk)]
        for z in range(brick_z):
            here = pair == z
            for k in range(per_chunk):
                v = brick[z + 1, pl.ds(base + ROWS * k, ROWS), :]
                packed[k] = jnp.where(here, pltpu.roll(v, 2 * z + 1, 1), packed[k])
        half = pl.multiple_of(chunk * (span // 2), ROWS)
        for k in range(0, per_chunk, 2):
            a, b = packed[k], packed[k + 1]
            at = pl.ds(half + ROWS * (k // 2), ROWS)
            x_out[0, at, :] = jnp.where(even, pltpu.roll(a, LANES - 1, 1), b)
            x_out[1, at, :] = jnp.where(even, a, pltpu.roll(b, 1, 1))
        return carry

    lax.fori_loop(0, CHUNKS, pack, 0)
    y_out[0] = brick[pl.ds(1, brick_z), ROWS, :]
    y_out[1] = brick[pl.ds(1, brick_z), ROWS + brick_y - 1, :]

    greeted = layers - 1
    for _, place, size in sides:
        greeted = greeted + jnp.where(place > 0, 1, 0) + jnp.where(place < size - 1, 1, 0)
    pl.semaphore_wait(barrier, greeted)

    data = pl.ds(ROWS, brick_y)
    halos = []
    for number, (axis, place, size, down, up) in enumerate(
        (
            ("ix", ix, nx, (x_out.at[0], x_in.at[1]), (x_out.at[1], x_in.at[0])),
            ("iy", iy, ny, (y_out.at[0], y_in.at[1]), (y_out.at[1], y_in.at[0])),
            (
                "depth",
                me,
                layers,
                (density.at[0], brick.at[brick_z + 1, data, :]),
                (density.at[brick_z - 1], brick.at[0, data, :]),
            ),
        )
    ):
        lower, upper = place > 0, place < size - 1
        for way, (go, come, (source, target), step) in enumerate(
            ((lower, upper, down, -1), (upper, lower, up, 1))
        ):
            copy = pltpu.make_async_remote_copy(
                src_ref=source,
                dst_ref=target,
                send_sem=halo_send.at[2 * number + way],
                recv_sem=halo_recv.at[2 * number + way],
                device_id={axis: place + step},
                device_id_type=MESH,
            )
            halos.append((copy, go, come, target))
    for copy, go, come, target in halos:

        @pl.when(go)
        def _():
            copy.start()

        @pl.when(jnp.logical_not(come))
        def _():
            target[...] = jnp.zeros(target.shape, jnp.float32)

    for copy in coeffs:
        copy.wait()
    root = math.sqrt(3.0 / (brick_z * layers) * math.log2(math.e))
    o0, o1, o2, o3 = (opacity_s[k] * (root / 4.0**k) for k in range(4))
    lx, ly, lz = (0.7 * light_s[k] for k in range(3))
    squares = []
    for channel in range(3):
        c0, c1, c2, c3 = (color_s[channel, k] for k in range(4))
        squares.append(
            [
                c0 * c0,
                2.0 * c0 * c1 / 4.0,
                (2.0 * c0 * c2 + c1 * c1) / 16.0,
                2.0 * (c0 * c3 + c1 * c2) / 64.0,
                (2.0 * c1 * c3 + c2 * c2) / 256.0,
                2.0 * c2 * c3 / 1024.0,
                c3 * c3 / 4096.0,
            ]
        )

    for copy, go, come, target in halos:

        @pl.when(come)
        def _():
            copy.wait_recv()

    def unpack(k, carry):
        at = pl.ds(pl.multiple_of(ROWS * k, ROWS), ROWS)
        left, right = x_in[0, at, :], x_in[1, at, :]
        first = pl.multiple_of(2 * ROWS * k, ROWS)
        x_halo[pl.ds(first, ROWS), :] = jnp.where(even, left, pltpu.roll(right, 1, 1))
        x_halo[pl.ds(first + ROWS, ROWS), :] = jnp.where(
            even, pltpu.roll(left, LANES - 1, 1), right
        )
        return carry

    lax.fori_loop(0, blocks // 2, unpack, 0)
    brick[pl.ds(1, brick_z), ROWS - 1, :] = y_in[0]
    brick[pl.ds(1, brick_z), ROWS + brick_y, :] = y_in[1]

    is_first, is_last = lane == 0, lane == LANES - 1

    def part_copy(block):
        return pltpu.make_async_remote_copy(
            src_ref=sent.at[block],
            dst_ref=parts.at[me],
            send_sem=part_send.at[block],
            recv_sem=part_recv.at[me],
            device_id={"depth": block},
            device_id_type=MESH,
        )

    def cast(block):
        row = pl.multiple_of(ROWS * block, ROWS)
        halo = x_halo[pl.ds(row, ROWS), :]

        zero = jnp.zeros((ROWS, LANES), jnp.float32)
        total, clear, moments = zero, zero + 1.0, [zero] * 7
        for z in range(brick_z):
            v = brick[z + 1, pl.ds(row + ROWS, ROWS), :]
            edge = pltpu.roll(halo, LANES - (2 * z + 1), 1)
            gx = pltpu.roll(jnp.where(is_first, edge, v), LANES - 1, 1) - pltpu.roll(
                jnp.where(is_last, edge, v), 1, 1
            )
            gy = (
                brick[z + 1, pl.ds(row + ROWS + 1, ROWS), :]
                - brick[z + 1, pl.ds(row + ROWS - 1, ROWS), :]
            )
            gz = brick[z + 2, pl.ds(row + ROWS, ROWS), :] - brick[z, pl.ds(row + ROWS, ROWS), :]
            facing = gx * lx + gy * ly + gz * lz
            norm = (gx * gx + gy * gy) + (gz * gz + 4.0)
            shading = jnp.abs(facing) * lax.rsqrt(norm) + 0.3
            p = ((o3 * v + o2) * v + o1) * v + o0
            total = total - p * p
            after = jnp.exp2(total)
            weight = (clear - after) * shading
            clear = after
            moments[0] = moments[0] + weight
            for degree in range(1, 7):
                weight = weight * v
                moments[degree] = moments[degree] + weight
        for channel in range(3):
            q = squares[channel]
            value = q[0] * moments[0]
            for degree in range(1, 7):
                value = value + q[degree] * moments[degree]
            sent[block, channel] = value
        sent[block, 3] = clear

    def others(step, carry):
        half = (step + 1) // 2
        hop = jnp.where(lax.rem(step, 2) == 0, layers // 2 + half, layers // 2 - half)
        block = lax.rem(me + hop, layers)
        cast(block)
        part_copy(block).start()
        return carry

    lax.fori_loop(0, layers - 1, others, 0)
    cast(me)

    def composite(layer, carry):
        red, green, blue, clear = carry

        @pl.when(layer != me)
        def _():
            pltpu.make_async_remote_copy(
                src_ref=sent.at[layer],
                dst_ref=parts.at[layer],
                send_sem=part_send.at[layer],
                recv_sem=part_recv.at[layer],
                device_id={"depth": layer},
                device_id_type=MESH,
            ).wait_recv()

        @pl.when(layer == me)
        def _():
            parts[layer] = sent[layer]

        return (
            red + clear * parts[layer, 0],
            green + clear * parts[layer, 1],
            blue + clear * parts[layer, 2],
            clear * parts[layer, 3],
        )

    zero = jnp.zeros((ROWS, LANES), jnp.float32)
    result = lax.fori_loop(0, layers, composite, (zero, zero, zero, zero + 1.0))
    for channel in range(4):
        image[channel] = result[channel]

    def finish(step, carry):
        part_copy(lax.rem(me + step, layers)).wait_send()
        return carry

    lax.fori_loop(1, layers, finish, 0)
    for copy, go, come, target in halos:

        @pl.when(go)
        def _():
            copy.wait_send()


def per_device(density, color_coeffs, opacity_coeffs, light):
    layers = lax.axis_size("depth")
    brick_z, brick_y, brick_x = density.shape
    blocks = brick_y // ROWS
    f32 = jnp.float32
    return pl.pallas_call(
        functools.partial(kernel, layers),
        out_shape=jax.ShapeDtypeStruct((4, ROWS, brick_x), f32),
        in_specs=[pl.BlockSpec(memory_space=pltpu.HBM)] * 4,
        out_specs=pl.BlockSpec(memory_space=pltpu.VMEM),
        scratch_shapes=[
            pltpu.VMEM((brick_z + 2, brick_y + 2 * ROWS, brick_x), f32),
            pltpu.VMEM((2, brick_y // 2, LANES), f32),
            pltpu.VMEM((2, brick_y // 2, LANES), f32),
            pltpu.VMEM((2, brick_z, LANES), f32),
            pltpu.VMEM((2, brick_z, LANES), f32),
            pltpu.VMEM((brick_y, LANES), f32),
            pltpu.VMEM((blocks, 4, ROWS, LANES), f32),
            pltpu.VMEM((layers, 4, ROWS, LANES), f32),
            pltpu.SMEM((3, 4), f32),
            pltpu.SMEM((4,), f32),
            pltpu.SMEM((3,), f32),
            pltpu.SemaphoreType.DMA((CHUNKS,)),
            pltpu.SemaphoreType.DMA((3,)),
            pltpu.SemaphoreType.DMA((6,)),
            pltpu.SemaphoreType.DMA((6,)),
            pltpu.SemaphoreType.DMA((blocks,)),
            pltpu.SemaphoreType.DMA((layers,)),
        ],
        compiler_params=pltpu.CompilerParams(
            collective_id=0, has_side_effects=True, vmem_limit_bytes=24 << 20
        ),
    )(density, color_coeffs, opacity_coeffs, light)


def solution(mesh):
    return jax.shard_map(
        per_device,
        mesh=mesh,
        in_specs=(P("depth", "iy", "ix"), P(), P(), P()),
        out_specs=P(None, ("iy", "depth"), "ix"),
        check_vma=False,
    )
```

```python
import functools
import math

import jax
import jax.numpy as jnp
from jax import lax
from jax.experimental import pallas as pl
from jax.experimental.pallas import tpu as pltpu
from jax.sharding import PartitionSpec as P

MESH = pl.DeviceIdType.MESH
LANES = 128
ROWS = 8
CHUNKS = 4


def kernel(
    layers,
    density,
    color,
    opacity,
    light,
    image,
    brick,
    opaque,
    x_out,
    x_in,
    y_out,
    y_in,
    x_halo,
    sent,
    parts,
    sent_clear,
    clears,
    color_s,
    opacity_s,
    light_s,
    load_sem,
    coeff_sem,
    halo_send,
    halo_recv,
    part_send,
    part_recv,
    clear_send,
    clear_recv,
):
    brick_z, brick_y, _ = density.shape
    blocks = brick_y // ROWS
    ix, nx = lax.axis_index("ix"), lax.axis_size("ix")
    iy, ny = lax.axis_index("iy"), lax.axis_size("iy")
    me = lax.axis_index("depth")

    barrier = pltpu.get_barrier_semaphore()
    sides = (("ix", ix, nx), ("iy", iy, ny))

    def greet(step, carry):
        pl.semaphore_signal(
            barrier, inc=1, device_id={"depth": lax.rem(me + step, layers)}, device_id_type=MESH
        )
        return carry

    lax.fori_loop(1, layers, greet, 0)
    for axis, place, size in sides:

        @pl.when(place > 0)
        def _():
            pl.semaphore_signal(barrier, inc=1, device_id={axis: place - 1}, device_id_type=MESH)

        @pl.when(place < size - 1)
        def _():
            pl.semaphore_signal(barrier, inc=1, device_id={axis: place + 1}, device_id_type=MESH)

    span = brick_y // CHUNKS

    def load(chunk):
        return pltpu.make_async_copy(
            density.at[:, pl.ds(chunk * span, span), :],
            brick.at[pl.ds(1, brick_z), pl.ds(ROWS + chunk * span, span), :],
            load_sem.at[chunk],
        )

    coeffs = [
        pltpu.make_async_copy(source, target, coeff_sem.at[number])
        for number, (source, target) in enumerate(
            ((opacity, opacity_s), (color, color_s), (light, light_s))
        )
    ]
    for copy in coeffs:
        copy.start()
    for chunk in range(CHUNKS):
        load(chunk).start()
    for copy in coeffs:
        copy.wait()
    root = math.sqrt(3.0 / (brick_z * layers) * math.log2(math.e))
    o0, o1, o2, o3 = (opacity_s[k] * (root / 4.0**k) for k in range(4))
    lx, ly, lz = (0.7 * light_s[k] for k in range(3))
    squares = []
    for channel in range(3):
        c0, c1, c2, c3 = (color_s[channel, k] for k in range(4))
        squares.append(
            [
                c0 * c0,
                2.0 * c0 * c1 / 4.0,
                (2.0 * c0 * c2 + c1 * c1) / 16.0,
                2.0 * (c0 * c3 + c1 * c2) / 64.0,
                (2.0 * c1 * c3 + c2 * c2) / 256.0,
                2.0 * c2 * c3 / 1024.0,
                c3 * c3 / 4096.0,
            ]
        )

    lane = lax.broadcasted_iota(jnp.int32, (ROWS, LANES), 1)
    even = lax.rem(lane, 2) == 0
    pair = lane // 2
    per_chunk = blocks // CHUNKS
    zero = jnp.zeros((ROWS, LANES), jnp.float32)

    def first_pass(chunk, carry):
        load(chunk).wait()
        base = pl.multiple_of(ROWS + chunk * span, ROWS)
        packed = [zero] * per_chunk
        for z in range(brick_z):
            here = pair == z
            for k in range(per_chunk):
                v = brick[z + 1, pl.ds(base + ROWS * k, ROWS), :]
                packed[k] = jnp.where(here, pltpu.roll(v, 2 * z + 1, 1), packed[k])
        half = pl.multiple_of(chunk * (span // 2), ROWS)
        for k in range(0, per_chunk, 2):
            a, b = packed[k], packed[k + 1]
            at = pl.ds(half + ROWS * (k // 2), ROWS)
            x_out[0, at, :] = jnp.where(even, pltpu.roll(a, LANES - 1, 1), b)
            x_out[1, at, :] = jnp.where(even, a, pltpu.roll(b, 1, 1))

        def hide(k, carry):
            row = pl.multiple_of(base + ROWS * k, ROWS)
            total, clear = zero, zero + 1.0
            for z in range(brick_z):
                v = brick[z + 1, pl.ds(row, ROWS), :]
                p = ((o3 * v + o2) * v + o1) * v + o0
                total = total - p * p
                after = jnp.exp2(total)
                opaque[z, pl.ds(row - ROWS, ROWS), :] = clear - after
                clear = after
            sent_clear[chunk * per_chunk + k] = clear
            return carry

        lax.fori_loop(0, per_chunk, hide, 0)
        return carry

    lax.fori_loop(0, CHUNKS, first_pass, 0)
    y_out[0] = brick[pl.ds(1, brick_z), ROWS, :]
    y_out[1] = brick[pl.ds(1, brick_z), ROWS + brick_y - 1, :]

    greeted = layers - 1
    for _, place, size in sides:
        greeted = greeted + jnp.where(place > 0, 1, 0) + jnp.where(place < size - 1, 1, 0)
    pl.semaphore_wait(barrier, greeted)

    data = pl.ds(ROWS, brick_y)
    halos = []
    for number, (axis, place, size, down, up) in enumerate(
        (
            (
                "depth",
                me,
                layers,
                (brick.at[1, data, :], brick.at[brick_z + 1, data, :]),
                (brick.at[brick_z, data, :], brick.at[0, data, :]),
            ),
            ("ix", ix, nx, (x_out.at[0], x_in.at[1]), (x_out.at[1], x_in.at[0])),
            ("iy", iy, ny, (y_out.at[0], y_in.at[1]), (y_out.at[1], y_in.at[0])),
        )
    ):
        lower, upper = place > 0, place < size - 1
        for way, (go, come, (source, target), step) in enumerate(
            ((lower, upper, down, -1), (upper, lower, up, 1))
        ):
            copy = pltpu.make_async_remote_copy(
                src_ref=source,
                dst_ref=target,
                send_sem=halo_send.at[2 * number + way],
                recv_sem=halo_recv.at[2 * number + way],
                device_id={axis: place + step},
                device_id_type=MESH,
            )
            halos.append((copy, go, come, target))
    for copy, go, come, target in halos:

        @pl.when(go)
        def _():
            copy.start()

        @pl.when(jnp.logical_not(come))
        def _():
            target[...] = jnp.zeros(target.shape, jnp.float32)

    def clear_copy(block, layer):
        return pltpu.make_async_remote_copy(
            src_ref=sent_clear.at[block],
            dst_ref=clears.at[layer],
            send_sem=clear_send.at[block],
            recv_sem=clear_recv.at[layer],
            device_id={"depth": block},
            device_id_type=MESH,
        )

    def part_copy(block, layer):
        return pltpu.make_async_remote_copy(
            src_ref=sent.at[block],
            dst_ref=parts.at[layer],
            send_sem=part_send.at[block],
            recv_sem=part_recv.at[layer],
            device_id={"depth": block},
            device_id_type=MESH,
        )

    half = layers // 2
    ahead = jnp.minimum(me, half)
    beyond = half - 1 - me

    def order(step):
        later = step - ahead
        swing = jnp.where(lax.rem(later, 2) == 0, half + later // 2, half - (later + 1) // 2)
        hop = jnp.where(later <= 2 * beyond, swing, half - (later - beyond))
        behind = half + lax.rem(later + me - half + 1, half)
        return jnp.where(step < ahead, step, jnp.where(me < half, me + hop, behind))

    def send_clear(step, carry):
        block = order(step)

        @pl.when(block != me)
        def _():
            clear_copy(block, me).start()

        return carry

    lax.fori_loop(0, blocks, send_clear, 0)

    for copy, go, come, target in halos:

        @pl.when(come)
        def _():
            copy.wait_recv()

    def unpack(k, carry):
        at = pl.ds(pl.multiple_of(ROWS * k, ROWS), ROWS)
        left, right = x_in[0, at, :], x_in[1, at, :]
        first = pl.multiple_of(2 * ROWS * k, ROWS)
        x_halo[pl.ds(first, ROWS), :] = jnp.where(even, left, pltpu.roll(right, 1, 1))
        x_halo[pl.ds(first + ROWS, ROWS), :] = jnp.where(
            even, pltpu.roll(left, LANES - 1, 1), right
        )
        return carry

    lax.fori_loop(0, blocks // 2, unpack, 0)
    brick[pl.ds(1, brick_z), ROWS - 1, :] = y_in[0]
    brick[pl.ds(1, brick_z), ROWS + brick_y, :] = y_in[1]

    is_first, is_last = lane == 0, lane == LANES - 1

    def shade(block):
        row = pl.multiple_of(ROWS * block, ROWS)
        halo = x_halo[pl.ds(row, ROWS), :]
        moments = [zero] * 7
        for z in range(brick_z):
            v = brick[z + 1, pl.ds(row + ROWS, ROWS), :]
            edge = pltpu.roll(halo, LANES - (2 * z + 1), 1)
            gx = pltpu.roll(jnp.where(is_first, edge, v), LANES - 1, 1) - pltpu.roll(
                jnp.where(is_last, edge, v), 1, 1
            )
            gy = (
                brick[z + 1, pl.ds(row + ROWS + 1, ROWS), :]
                - brick[z + 1, pl.ds(row + ROWS - 1, ROWS), :]
            )
            gz = brick[z + 2, pl.ds(row + ROWS, ROWS), :] - brick[z, pl.ds(row + ROWS, ROWS), :]
            facing = gx * lx + gy * ly + gz * lz
            norm = (gx * gx + gy * gy) + (gz * gz + 4.0)
            shading = jnp.abs(facing) * lax.rsqrt(norm) + 0.3
            weight = opaque[z, pl.ds(row, ROWS), :] * shading
            moments[0] = moments[0] + weight
            for degree in range(1, 7):
                weight = weight * v
                moments[degree] = moments[degree] + weight
        for channel in range(3):
            q = squares[channel]
            value = q[0] * moments[0]
            for degree in range(1, 7):
                value = value + q[degree] * moments[degree]
            sent[block, channel] = value

    def each(step, carry):
        block = order(step)
        shade(block)

        @pl.when(block != me)
        def _():
            part_copy(block, me).start()

        return carry

    lax.fori_loop(0, blocks, each, 0)

    def composite(layer, carry):
        red, green, blue, clear = carry

        @pl.when(layer != me)
        def _():
            clear_copy(layer, layer).wait_recv()
            part_copy(layer, layer).wait_recv()

        @pl.when(layer == me)
        def _():
            clears[layer] = sent_clear[layer]
            parts[layer] = sent[layer]

        return (
            red + clear * parts[layer, 0],
            green + clear * parts[layer, 1],
            blue + clear * parts[layer, 2],
            clear * clears[layer],
        )

    result = lax.fori_loop(0, layers, composite, (zero, zero, zero, zero + 1.0))
    for channel in range(4):
        image[channel] = result[channel]

    def finish(step, carry):
        block = lax.rem(me + step, layers)
        clear_copy(block, me).wait_send()
        part_copy(block, me).wait_send()
        return carry

    lax.fori_loop(1, layers, finish, 0)
    for copy, go, come, target in halos:

        @pl.when(go)
        def _():
            copy.wait_send()


def per_device(density, color_coeffs, opacity_coeffs, light):
    layers = lax.axis_size("depth")
    brick_z, brick_y, brick_x = density.shape
    blocks = brick_y // ROWS
    f32 = jnp.float32
    dma = pltpu.SemaphoreType.DMA
    return pl.pallas_call(
        functools.partial(kernel, layers),
        out_shape=jax.ShapeDtypeStruct((4, ROWS, brick_x), f32),
        in_specs=[pl.BlockSpec(memory_space=pltpu.HBM)] * 4,
        out_specs=pl.BlockSpec(memory_space=pltpu.VMEM),
        scratch_shapes=[
            pltpu.VMEM((brick_z + 2, brick_y + 2 * ROWS, brick_x), f32),
            pltpu.VMEM((brick_z, brick_y, brick_x), f32),
            pltpu.VMEM((2, brick_y // 2, LANES), f32),
            pltpu.VMEM((2, brick_y // 2, LANES), f32),
            pltpu.VMEM((2, brick_z, LANES), f32),
            pltpu.VMEM((2, brick_z, LANES), f32),
            pltpu.VMEM((brick_y, LANES), f32),
            pltpu.VMEM((blocks, 3, ROWS, LANES), f32),
            pltpu.VMEM((layers, 3, ROWS, LANES), f32),
            pltpu.VMEM((blocks, ROWS, LANES), f32),
            pltpu.VMEM((layers, ROWS, LANES), f32),
            pltpu.SMEM((3, 4), f32),
            pltpu.SMEM((4,), f32),
            pltpu.SMEM((3,), f32),
            dma((CHUNKS,)),
            dma((3,)),
            dma((6,)),
            dma((6,)),
            dma((blocks,)),
            dma((layers,)),
            dma((blocks,)),
            dma((layers,)),
        ],
        compiler_params=pltpu.CompilerParams(
            collective_id=0, has_side_effects=True, vmem_limit_bytes=60 << 20
        ),
    )(density, color_coeffs, opacity_coeffs, light)


def solution(mesh):
    return jax.shard_map(
        per_device,
        mesh=mesh,
        in_specs=(P("depth", "iy", "ix"), P(), P(), P()),
        out_specs=P(None, ("iy", "depth"), "ix"),
        check_vma=False,
    )
```

```python
import functools
import math

import jax
import jax.numpy as jnp
from jax import lax
from jax.experimental import pallas as pl
from jax.experimental.pallas import tpu as pltpu
from jax.sharding import PartitionSpec as P

MESH = pl.DeviceIdType.MESH
LANES = 128
ROWS = 8
CHUNKS = 4


def kernel(
    layers,
    density,
    color,
    opacity,
    light,
    image,
    brick,
    opaque,
    x_out,
    x_in,
    y_out,
    y_in,
    x_halo,
    sent,
    parts,
    sent_clear,
    clears,
    color_s,
    opacity_s,
    light_s,
    load_sem,
    coeff_sem,
    halo_send,
    halo_recv,
    part_send,
    part_recv,
    clear_send,
    clear_recv,
):
    brick_z, brick_y, _ = density.shape
    blocks = brick_y // ROWS
    ix, nx = lax.axis_index("ix"), lax.axis_size("ix")
    iy, ny = lax.axis_index("iy"), lax.axis_size("iy")
    me = lax.axis_index("depth")

    barrier = pltpu.get_barrier_semaphore()
    sides = (("ix", ix, nx), ("iy", iy, ny))

    half = layers // 2

    def swing(step):
        return jnp.where(lax.rem(step, 2) == 0, half + step // 2, half - (step + 1) // 2)

    def greet(step, carry):
        other = lax.rem(me + swing(step), layers)
        pl.semaphore_signal(barrier, inc=1, device_id={"depth": other}, device_id_type=MESH)
        return carry

    lax.fori_loop(0, layers - 1, greet, 0)
    for axis, place, size in sides:

        @pl.when(place > 0)
        def _():
            pl.semaphore_signal(barrier, inc=1, device_id={axis: place - 1}, device_id_type=MESH)

        @pl.when(place < size - 1)
        def _():
            pl.semaphore_signal(barrier, inc=1, device_id={axis: place + 1}, device_id_type=MESH)

    span = brick_y // CHUNKS

    def load(chunk):
        return pltpu.make_async_copy(
            density.at[:, pl.ds(chunk * span, span), :],
            brick.at[pl.ds(1, brick_z), pl.ds(ROWS + chunk * span, span), :],
            load_sem.at[chunk],
        )

    coeffs = [
        pltpu.make_async_copy(source, target, coeff_sem.at[number])
        for number, (source, target) in enumerate(
            ((opacity, opacity_s), (color, color_s), (light, light_s))
        )
    ]
    for copy in coeffs:
        copy.start()
    for chunk in range(CHUNKS):
        load(chunk).start()
    for copy in coeffs:
        copy.wait()
    root = math.sqrt(3.0 / (brick_z * layers) * math.log2(math.e))
    o0, o1, o2, o3 = (opacity_s[k] * (root / 4.0**k) for k in range(4))
    lx, ly, lz = (0.7 * light_s[k] for k in range(3))
    squares = []
    for channel in range(3):
        c0, c1, c2, c3 = (color_s[channel, k] for k in range(4))
        squares.append(
            [
                c0 * c0,
                2.0 * c0 * c1 / 4.0,
                (2.0 * c0 * c2 + c1 * c1) / 16.0,
                2.0 * (c0 * c3 + c1 * c2) / 64.0,
                (2.0 * c1 * c3 + c2 * c2) / 256.0,
                2.0 * c2 * c3 / 1024.0,
                c3 * c3 / 4096.0,
            ]
        )

    lane = lax.broadcasted_iota(jnp.int32, (ROWS, LANES), 1)
    even = lax.rem(lane, 2) == 0
    pair = lane // 2
    per_chunk = blocks // CHUNKS
    zero = jnp.zeros((ROWS, LANES), jnp.float32)

    def first_pass(chunk, carry):
        load(chunk).wait()
        base = pl.multiple_of(ROWS + chunk * span, ROWS)
        packed = [zero] * per_chunk
        for z in range(brick_z):
            here = pair == z
            for k in range(per_chunk):
                v = brick[z + 1, pl.ds(base + ROWS * k, ROWS), :]
                packed[k] = jnp.where(here, pltpu.roll(v, 2 * z + 1, 1), packed[k])
        first = pl.multiple_of(chunk * (span // 2), ROWS)
        for k in range(0, per_chunk, 2):
            a, b = packed[k], packed[k + 1]
            at = pl.ds(first + ROWS * (k // 2), ROWS)
            x_out[0, at, :] = jnp.where(even, pltpu.roll(a, LANES - 1, 1), b)
            x_out[1, at, :] = jnp.where(even, a, pltpu.roll(b, 1, 1))
        return carry

    def hide(block, carry):
        row = pl.multiple_of(ROWS * block, ROWS)
        total, clear = zero, zero + 1.0
        for z in range(brick_z):
            v = brick[z + 1, pl.ds(row + ROWS, ROWS), :]
            p = ((o3 * v + o2) * v + o1) * v + o0
            total = total - p * p
            after = jnp.exp2(total)
            opaque[z, pl.ds(row, ROWS), :] = clear - after
            clear = after
        sent_clear[block] = clear
        return carry

    lax.fori_loop(0, CHUNKS, first_pass, 0)
    y_out[0] = brick[pl.ds(1, brick_z), ROWS, :]
    y_out[1] = brick[pl.ds(1, brick_z), ROWS + brick_y - 1, :]

    early = jnp.where(me < half, blocks, 4 * jnp.maximum(0, jnp.abs(me - half - 3) - 1))
    lax.fori_loop(0, early, hide, 0)

    greeted = layers - 1
    for _, place, size in sides:
        greeted = greeted + jnp.where(place > 0, 1, 0) + jnp.where(place < size - 1, 1, 0)
    pl.semaphore_wait(barrier, greeted)

    def plane(chunk):
        return pl.ds(ROWS + chunk * span, span)

    lanes = [
        (
            "depth",
            me,
            layers,
            (brick.at[1, plane(k), :], brick.at[brick_z + 1, plane(k), :]),
            (brick.at[brick_z, plane(k), :], brick.at[0, plane(k), :]),
        )
        for k in range(CHUNKS)
    ]
    lanes[1:1] = [
        ("ix", ix, nx, (x_out.at[0], x_in.at[1]), (x_out.at[1], x_in.at[0])),
        ("iy", iy, ny, (y_out.at[0], y_in.at[1]), (y_out.at[1], y_in.at[0])),
    ]
    halos = []
    for number, (axis, place, size, down, up) in enumerate(lanes):
        lower, upper = place > 0, place < size - 1
        for way, (go, come, (source, target), step) in enumerate(
            ((lower, upper, down, -1), (upper, lower, up, 1))
        ):
            copy = pltpu.make_async_remote_copy(
                src_ref=source,
                dst_ref=target,
                send_sem=halo_send.at[2 * number + way],
                recv_sem=halo_recv.at[2 * number + way],
                device_id={axis: place + step},
                device_id_type=MESH,
            )
            halos.append((copy, go, come, target))
    for copy, go, come, target in halos:

        @pl.when(go)
        def _():
            copy.start()

        @pl.when(jnp.logical_not(come))
        def _():
            target[...] = jnp.zeros(target.shape, jnp.float32)

    lax.fori_loop(early, blocks, hide, 0)

    def clear_copy(block, layer):
        return pltpu.make_async_remote_copy(
            src_ref=sent_clear.at[block],
            dst_ref=clears.at[layer],
            send_sem=clear_send.at[block],
            recv_sem=clear_recv.at[layer],
            device_id={"depth": block},
            device_id_type=MESH,
        )

    def part_copy(block, layer):
        return pltpu.make_async_remote_copy(
            src_ref=sent.at[block],
            dst_ref=parts.at[layer],
            send_sem=part_send.at[block],
            recv_sem=part_recv.at[layer],
            device_id={"depth": block},
            device_id_type=MESH,
        )

    ahead = jnp.minimum(me, half)
    beyond = half - 1 - me

    def order(step):
        later = step - ahead
        hop = jnp.where(later <= 2 * beyond, swing(later), half - (later - beyond))
        behind = half + lax.rem(later + me - half + 1, half)
        return jnp.where(step < ahead, step, jnp.where(me < half, me + hop, behind))

    def send_clear(step, carry):
        block = order(step)

        @pl.when(block != me)
        def _():
            clear_copy(block, me).start()

        return carry

    lax.fori_loop(0, blocks, send_clear, 0)

    def arrive(some):
        for copy, _, come, _ in some:

            @pl.when(come)
            def _():
                copy.wait_recv()

    arrive(halos[:6])

    def unpack(k, carry):
        at = pl.ds(pl.multiple_of(ROWS * k, ROWS), ROWS)
        left, right = x_in[0, at, :], x_in[1, at, :]
        first = pl.multiple_of(2 * ROWS * k, ROWS)
        x_halo[pl.ds(first, ROWS), :] = jnp.where(even, left, pltpu.roll(right, 1, 1))
        x_halo[pl.ds(first + ROWS, ROWS), :] = jnp.where(
            even, pltpu.roll(left, LANES - 1, 1), right
        )
        return carry

    lax.fori_loop(0, blocks // 2, unpack, 0)
    brick[pl.ds(1, brick_z), ROWS - 1, :] = y_in[0]
    brick[pl.ds(1, brick_z), ROWS + brick_y, :] = y_in[1]

    is_first, is_last = lane == 0, lane == LANES - 1

    def shade(block):
        row = pl.multiple_of(ROWS * block, ROWS)
        halo = x_halo[pl.ds(row, ROWS), :]
        moments = [zero] * 7
        for z in range(brick_z):
            v = brick[z + 1, pl.ds(row + ROWS, ROWS), :]
            edge = pltpu.roll(halo, LANES - (2 * z + 1), 1)
            gx = pltpu.roll(jnp.where(is_first, edge, v), LANES - 1, 1) - pltpu.roll(
                jnp.where(is_last, edge, v), 1, 1
            )
            gy = (
                brick[z + 1, pl.ds(row + ROWS + 1, ROWS), :]
                - brick[z + 1, pl.ds(row + ROWS - 1, ROWS), :]
            )
            gz = brick[z + 2, pl.ds(row + ROWS, ROWS), :] - brick[z, pl.ds(row + ROWS, ROWS), :]
            facing = gx * lx + gy * ly + gz * lz
            norm = (gx * gx + gy * gy) + (gz * gz + 4.0)
            shading = jnp.abs(facing) * lax.rsqrt(norm) + 0.3
            weight = opaque[z, pl.ds(row, ROWS), :] * shading
            moments[0] = moments[0] + weight
            for degree in range(1, 7):
                weight = weight * v
                moments[degree] = moments[degree] + weight
        for channel in range(3):
            q = squares[channel]
            value = q[0] * moments[0]
            for degree in range(1, 7):
                value = value + q[degree] * moments[degree]
            sent[block, channel] = value

    def each(step, carry):
        block = order(step)

        @pl.when(step == jnp.minimum(ahead, half // 2))
        def _():
            arrive(halos[6:8])

        @pl.when(step == ahead)
        def _():
            arrive(halos[8:])

        shade(block)

        @pl.when(block != me)
        def _():
            part_copy(block, me).start()

        return carry

    lax.fori_loop(0, blocks, each, 0)

    def composite(layer, carry):
        red, green, blue, clear = carry

        @pl.when(layer != me)
        def _():
            clear_copy(layer, layer).wait_recv()
            part_copy(layer, layer).wait_recv()

        @pl.when(layer == me)
        def _():
            clears[layer] = sent_clear[layer]
            parts[layer] = sent[layer]

        return (
            red + clear * parts[layer, 0],
            green + clear * parts[layer, 1],
            blue + clear * parts[layer, 2],
            clear * clears[layer],
        )

    result = lax.fori_loop(0, layers, composite, (zero, zero, zero, zero + 1.0))
    for channel in range(4):
        image[channel] = result[channel]

    def finish(step, carry):
        block = lax.rem(me + step, layers)
        clear_copy(block, me).wait_send()
        part_copy(block, me).wait_send()
        return carry

    lax.fori_loop(1, layers, finish, 0)
    for copy, go, come, target in halos:

        @pl.when(go)
        def _():
            copy.wait_send()


def per_device(*arguments):
    density = arguments[0]
    layers = lax.axis_size("depth")
    brick_z, brick_y, brick_x = density.shape
    blocks = brick_y // ROWS
    f32 = jnp.float32
    dma = pltpu.SemaphoreType.DMA
    return pl.pallas_call(
        functools.partial(kernel, layers),
        out_shape=jax.ShapeDtypeStruct((4, ROWS, brick_x), f32),
        in_specs=[pl.BlockSpec(memory_space=pltpu.HBM)] * 4,
        out_specs=pl.BlockSpec(memory_space=pltpu.VMEM),
        scratch_shapes=[
            pltpu.VMEM((brick_z + 2, brick_y + 2 * ROWS, brick_x), f32),
            pltpu.VMEM((brick_z, brick_y, brick_x), f32),
            pltpu.VMEM((2, brick_y // 2, LANES), f32),
            pltpu.VMEM((2, brick_y // 2, LANES), f32),
            pltpu.VMEM((2, brick_z, LANES), f32),
            pltpu.VMEM((2, brick_z, LANES), f32),
            pltpu.VMEM((brick_y, LANES), f32),
            pltpu.VMEM((blocks, 3, ROWS, LANES), f32),
            pltpu.VMEM((layers, 3, ROWS, LANES), f32),
            pltpu.VMEM((blocks, ROWS, LANES), f32),
            pltpu.VMEM((layers, ROWS, LANES), f32),
            pltpu.SMEM((3, 4), f32),
            pltpu.SMEM((4,), f32),
            pltpu.SMEM((3,), f32),
            dma((CHUNKS,)),
            dma((3,)),
            dma((2 * CHUNKS + 4,)),
            dma((2 * CHUNKS + 4,)),
            dma((blocks,)),
            dma((layers,)),
            dma((blocks,)),
            dma((layers,)),
        ],
        compiler_params=pltpu.CompilerParams(
            collective_id=0, has_side_effects=True, vmem_limit_bytes=32 << 20
        ),
    )(*(pltpu.with_memory_space_constraint(a, pltpu.HBM) for a in arguments))


def solution(mesh):
    return jax.shard_map(
        per_device,
        mesh=mesh,
        in_specs=(P("depth", "iy", "ix"), P(), P(), P()),
        out_specs=P(None, ("iy", "depth"), "ix"),
        check_vma=False,
    )
```

```python
import functools
import math

import jax
import jax.numpy as jnp
from jax import lax
from jax.experimental import pallas as pl
from jax.experimental.pallas import tpu as pltpu
from jax.sharding import PartitionSpec as P

MESH = pl.DeviceIdType.MESH
LANES = 128
ROWS = 8
CHUNKS = 4
BETWEEN = 2


def kernel(
    layers,
    density,
    color,
    opacity,
    light,
    image,
    brick,
    opaque,
    dots,
    norms,
    steps,
    x_out,
    x_in,
    y_out,
    y_in,
    x_halo,
    sent,
    parts,
    sent_clear,
    clears,
    color_s,
    opacity_s,
    light_s,
    load_sem,
    coeff_sem,
    halo_send,
    halo_recv,
    part_send,
    part_recv,
    clear_send,
    clear_recv,
):
    brick_z, brick_y, _ = density.shape
    blocks = brick_y // ROWS
    ix, nx = lax.axis_index("ix"), lax.axis_size("ix")
    iy, ny = lax.axis_index("iy"), lax.axis_size("iy")
    me = lax.axis_index("depth")

    barrier = pltpu.get_barrier_semaphore()
    sides = (("ix", ix, nx), ("iy", iy, ny))

    half = layers // 2

    def swing(step):
        return jnp.where(lax.rem(step, 2) == 0, half + step // 2, half - (step + 1) // 2)

    def greet(step, carry):
        other = lax.rem(me + swing(step), layers)
        pl.semaphore_signal(barrier, inc=1, device_id={"depth": other}, device_id_type=MESH)
        return carry

    lax.fori_loop(0, layers - 1, greet, 0)
    for axis, place, size in sides:

        @pl.when(place > 0)
        def _():
            pl.semaphore_signal(barrier, inc=1, device_id={axis: place - 1}, device_id_type=MESH)

        @pl.when(place < size - 1)
        def _():
            pl.semaphore_signal(barrier, inc=1, device_id={axis: place + 1}, device_id_type=MESH)

    span = brick_y // CHUNKS

    def load(chunk):
        return pltpu.make_async_copy(
            density.at[:, pl.ds(chunk * span, span), :],
            brick.at[pl.ds(1, brick_z), pl.ds(ROWS + chunk * span, span), :],
            load_sem.at[chunk],
        )

    coeffs = [
        pltpu.make_async_copy(source, target, coeff_sem.at[number])
        for number, (source, target) in enumerate(
            ((opacity, opacity_s), (color, color_s), (light, light_s))
        )
    ]
    for copy in coeffs:
        copy.start()
    for chunk in range(CHUNKS):
        load(chunk).start()
    for copy in coeffs:
        copy.wait()
    root = math.sqrt(3.0 / (brick_z * layers) * math.log2(math.e))
    o0, o1, o2, o3 = (opacity_s[k] * (root / 4.0**k) for k in range(4))
    lx, ly, lz = (0.7 * light_s[k] for k in range(3))
    squares = []
    for channel in range(3):
        c0, c1, c2, c3 = (color_s[channel, k] for k in range(4))
        squares.append(
            [
                c0 * c0,
                2.0 * c0 * c1 / 4.0,
                (2.0 * c0 * c2 + c1 * c1) / 16.0,
                2.0 * (c0 * c3 + c1 * c2) / 64.0,
                (2.0 * c1 * c3 + c2 * c2) / 256.0,
                2.0 * c2 * c3 / 1024.0,
                c3 * c3 / 4096.0,
            ]
        )

    lane = lax.broadcasted_iota(jnp.int32, (ROWS, LANES), 1)
    even = lax.rem(lane, 2) == 0
    pair = lane // 2
    per_chunk = blocks // CHUNKS
    zero = jnp.zeros((ROWS, LANES), jnp.float32)

    def first_pass(chunk, carry):
        load(chunk).wait()
        base = pl.multiple_of(ROWS + chunk * span, ROWS)
        packed = [zero] * per_chunk
        for z in range(brick_z):
            here = pair == z
            for k in range(per_chunk):
                v = brick[z + 1, pl.ds(base + ROWS * k, ROWS), :]
                packed[k] = jnp.where(here, pltpu.roll(v, 2 * z + 1, 1), packed[k])
        first = pl.multiple_of(chunk * (span // 2), ROWS)
        for k in range(0, per_chunk, 2):
            a, b = packed[k], packed[k + 1]
            at = pl.ds(first + ROWS * (k // 2), ROWS)
            x_out[0, at, :] = jnp.where(even, pltpu.roll(a, LANES - 1, 1), b)
            x_out[1, at, :] = jnp.where(even, a, pltpu.roll(b, 1, 1))
        return carry

    def hide(block, carry):
        row = pl.multiple_of(ROWS * block, ROWS)
        total, clear = zero, zero + 1.0
        for z in range(brick_z):
            v = brick[z + 1, pl.ds(row + ROWS, ROWS), :]
            p = ((o3 * v + o2) * v + o1) * v + o0
            total = total - p * p
            after = jnp.exp2(total)
            opaque[z, pl.ds(row, ROWS), :] = clear - after
            clear = after
        sent_clear[block] = clear
        return carry

    lax.fori_loop(0, CHUNKS, first_pass, 0)
    y_out[0] = brick[pl.ds(1, brick_z), ROWS, :]
    y_out[1] = brick[pl.ds(1, brick_z), ROWS + brick_y - 1, :]

    def slopes(block, z):
        row = pl.multiple_of(ROWS * block, ROWS)
        gy = (
            brick[z + 1, pl.ds(row + ROWS + 1, ROWS), :]
            - brick[z + 1, pl.ds(row + ROWS - 1, ROWS), :]
        )
        gz = brick[z + 2, pl.ds(row + ROWS, ROWS), :] - brick[z, pl.ds(row + ROWS, ROWS), :]
        return gy * ly + gz * lz, gy * gy + (gz * gz + 4.0)

    def across(block, z):
        v = brick[z + 1, pl.ds(pl.multiple_of(ROWS * block + ROWS, ROWS), ROWS), :]
        return pltpu.roll(v, LANES - 1, 1) - pltpu.roll(v, 1, 1)

    def slope(block, carry=0):
        at = pl.ds(pl.multiple_of(ROWS * block, ROWS), ROWS)
        for z in range(1, brick_z - 1):
            dots[z, at, :], norms[z, at, :] = slopes(block, z)
            steps[z, at, :] = across(block, z)
        return carry

    early = jnp.where(me < half, blocks, 4 * jnp.maximum(0, jnp.abs(me - half - 3) - 1))
    lax.fori_loop(0, early, hide, 0)
    sloped = jnp.where(me < half, blocks - 1, 1)
    lax.fori_loop(1, sloped, slope, 0)

    greeted = layers - 1
    for _, place, size in sides:
        greeted = greeted + jnp.where(place > 0, 1, 0) + jnp.where(place < size - 1, 1, 0)
    pl.semaphore_wait(barrier, greeted)

    def plane(chunk):
        return pl.ds(ROWS + chunk * span, span)

    lanes = [
        (
            "depth",
            me,
            layers,
            (brick.at[1, plane(k), :], brick.at[brick_z + 1, plane(k), :]),
            (brick.at[brick_z, plane(k), :], brick.at[0, plane(k), :]),
        )
        for k in range(CHUNKS)
    ]
    lanes[1:1] = [
        ("ix", ix, nx, (x_out.at[0], x_in.at[1]), (x_out.at[1], x_in.at[0])),
        ("iy", iy, ny, (y_out.at[0], y_in.at[1]), (y_out.at[1], y_in.at[0])),
    ]
    halos = []
    for number, (axis, place, size, down, up) in enumerate(lanes):
        lower, upper = place > 0, place < size - 1
        for way, (go, come, (source, target), step) in enumerate(
            ((lower, upper, down, -1), (upper, lower, up, 1))
        ):
            copy = pltpu.make_async_remote_copy(
                src_ref=source,
                dst_ref=target,
                send_sem=halo_send.at[2 * number + way],
                recv_sem=halo_recv.at[2 * number + way],
                device_id={axis: place + step},
                device_id_type=MESH,
            )
            halos.append((copy, go, come, target))
    for copy, go, come, target in halos:

        @pl.when(go)
        def _():
            copy.start()

        @pl.when(jnp.logical_not(come))
        def _():
            target[...] = jnp.zeros(target.shape, jnp.float32)

    lax.fori_loop(early, blocks, hide, 0)

    def clear_copy(block, layer):
        return pltpu.make_async_remote_copy(
            src_ref=sent_clear.at[block],
            dst_ref=clears.at[layer],
            send_sem=clear_send.at[block],
            recv_sem=clear_recv.at[layer],
            device_id={"depth": block},
            device_id_type=MESH,
        )

    def part_copy(block, layer):
        return pltpu.make_async_remote_copy(
            src_ref=sent.at[block],
            dst_ref=parts.at[layer],
            send_sem=part_send.at[block],
            recv_sem=part_recv.at[layer],
            device_id={"depth": block},
            device_id_type=MESH,
        )

    ahead = jnp.minimum(me, half // 2)
    second = jnp.clip(me - half // 2, 0, half // 2)
    beyond = half - 1 - me

    def order(step):
        place = step - ahead
        later = place - jnp.where(place >= BETWEEN + second, second, 0)
        hop = jnp.where(later <= 2 * beyond, swing(later), half - (later - beyond))
        behind = half + lax.rem(later + me - half + 1, half)
        rest = jnp.where(me < half, me + hop, behind)
        inside = (place >= BETWEEN) & (place < BETWEEN + second)
        return jnp.where(step < ahead, step, jnp.where(inside, half // 2 + place - BETWEEN, rest))

    def send_clear(step, carry):
        block = order(step)

        @pl.when(block != me)
        def _():
            clear_copy(block, me).start()

        return carry

    lax.fori_loop(0, blocks, send_clear, 0)

    def arrive(some):
        for copy, _, come, _ in some:

            @pl.when(come)
            def _():
                copy.wait_recv()

    lax.fori_loop(sloped, blocks - 1, slope, 0)
    arrive(halos[4:6])
    brick[pl.ds(1, brick_z), ROWS - 1, :] = y_in[0]
    brick[pl.ds(1, brick_z), ROWS + brick_y, :] = y_in[1]
    slope(0)
    slope(blocks - 1)
    arrive(halos[:4])

    def unpack(k, carry):
        at = pl.ds(pl.multiple_of(ROWS * k, ROWS), ROWS)
        last = x_in[1, at, :] - x_out[0, at, :]
        first = x_out[1, at, :] - x_in[0, at, :]
        row = pl.multiple_of(2 * ROWS * k, ROWS)
        x_halo[pl.ds(row, ROWS), :] = jnp.where(even, last, pltpu.roll(first, 1, 1))
        x_halo[pl.ds(row + ROWS, ROWS), :] = jnp.where(
            even, pltpu.roll(last, LANES - 1, 1), first
        )
        return carry

    lax.fori_loop(0, blocks // 2, unpack, 0)
    is_edge = (lane == 0) | (lane == LANES - 1)

    def shade(block):
        row = pl.multiple_of(ROWS * block, ROWS)
        at = pl.ds(row, ROWS)
        halo = x_halo[at, :]
        moments = [zero] * 7
        for z in range(brick_z):
            v = brick[z + 1, pl.ds(row + ROWS, ROWS), :]
            edge = pltpu.roll(halo, LANES - (2 * z + 1), 1)
            if z in (0, brick_z - 1):
                dot, norm = slopes(block, z)
                gx = across(block, z)
            else:
                dot, norm, gx = dots[z, at, :], norms[z, at, :], steps[z, at, :]
            gx = gx + jnp.where(is_edge, edge, 0.0)
            shading = jnp.abs(gx * lx + dot) * lax.rsqrt(gx * gx + norm) + 0.3
            weight = opaque[z, at, :] * shading
            moments[0] = moments[0] + weight
            for degree in range(1, 7):
                weight = weight * v
                moments[degree] = moments[degree] + weight
        for channel in range(3):
            q = squares[channel]
            value = q[0] * moments[0]
            for degree in range(1, 7):
                value = value + q[degree] * moments[degree]
            sent[block, channel] = value

    def each(step, carry):
        block = order(step)

        @pl.when(step == ahead)
        def _():
            arrive(halos[6:])

        shade(block)

        @pl.when(block != me)
        def _():
            part_copy(block, me).start()

        return carry

    lax.fori_loop(0, blocks, each, 0)

    def composite(layer, carry):
        red, green, blue, clear = carry

        @pl.when(layer != me)
        def _():
            clear_copy(layer, layer).wait_recv()
            part_copy(layer, layer).wait_recv()

        @pl.when(layer == me)
        def _():
            clears[layer] = sent_clear[layer]
            parts[layer] = sent[layer]

        return (
            red + clear * parts[layer, 0],
            green + clear * parts[layer, 1],
            blue + clear * parts[layer, 2],
            clear * clears[layer],
        )

    result = lax.fori_loop(0, layers, composite, (zero, zero, zero, zero + 1.0))
    for channel in range(4):
        image[channel] = result[channel]

    def finish(step, carry):
        block = lax.rem(me + step, layers)
        clear_copy(block, me).wait_send()
        part_copy(block, me).wait_send()
        return carry

    lax.fori_loop(1, layers, finish, 0)
    for copy, go, come, target in halos:

        @pl.when(go)
        def _():
            copy.wait_send()


def per_device(*arguments):
    density = arguments[0]
    layers = lax.axis_size("depth")
    brick_z, brick_y, brick_x = density.shape
    blocks = brick_y // ROWS
    f32 = jnp.float32
    dma = pltpu.SemaphoreType.DMA
    return pl.pallas_call(
        functools.partial(kernel, layers),
        out_shape=jax.ShapeDtypeStruct((4, ROWS, brick_x), f32),
        in_specs=[pl.BlockSpec(memory_space=pltpu.HBM)] * 4,
        out_specs=pl.BlockSpec(memory_space=pltpu.VMEM),
        scratch_shapes=[
            pltpu.VMEM((brick_z + 2, brick_y + 2 * ROWS, brick_x), f32),
            *[pltpu.VMEM((brick_z, brick_y, brick_x), f32)] * 4,
            pltpu.VMEM((2, brick_y // 2, LANES), f32),
            pltpu.VMEM((2, brick_y // 2, LANES), f32),
            pltpu.VMEM((2, brick_z, LANES), f32),
            pltpu.VMEM((2, brick_z, LANES), f32),
            pltpu.VMEM((brick_y, LANES), f32),
            pltpu.VMEM((blocks, 3, ROWS, LANES), f32),
            pltpu.VMEM((layers, 3, ROWS, LANES), f32),
            pltpu.VMEM((blocks, ROWS, LANES), f32),
            pltpu.VMEM((layers, ROWS, LANES), f32),
            pltpu.SMEM((3, 4), f32),
            pltpu.SMEM((4,), f32),
            pltpu.SMEM((3,), f32),
            dma((CHUNKS,)),
            dma((3,)),
            dma((2 * CHUNKS + 4,)),
            dma((2 * CHUNKS + 4,)),
            dma((blocks,)),
            dma((layers,)),
            dma((blocks,)),
            dma((layers,)),
        ],
        compiler_params=pltpu.CompilerParams(
            collective_id=0, has_side_effects=True, vmem_limit_bytes=32 << 20
        ),
    )(*(pltpu.with_memory_space_constraint(a, pltpu.HBM) for a in arguments))


def solution(mesh):
    return jax.shard_map(
        per_device,
        mesh=mesh,
        in_specs=(P("depth", "iy", "ix"), P(), P(), P()),
        out_specs=P(None, ("iy", "depth"), "ix"),
        check_vma=False,
    )
```

```python
import functools
import math

import jax
import jax.numpy as jnp
from jax import lax
from jax.experimental import pallas as pl
from jax.experimental.pallas import tpu as pltpu
from jax.sharding import PartitionSpec as P

MESH = pl.DeviceIdType.MESH
LANES = 128
ROWS = 8
CHUNKS = 4
BETWEEN = 2
NEAR = 4


def kernel(
    layers,
    density,
    color,
    opacity,
    light,
    image,
    brick,
    opaque,
    dots,
    norms,
    steps,
    x_out,
    x_in,
    y_out,
    y_in,
    x_halo,
    sent,
    parts,
    sent_clear,
    clears,
    color_s,
    opacity_s,
    light_s,
    load_sem,
    coeff_sem,
    halo_send,
    halo_recv,
    part_send,
    part_recv,
    clear_send,
    clear_recv,
    open_sem,
):
    brick_z, brick_y, _ = density.shape
    blocks = brick_y // ROWS
    ix, nx = lax.axis_index("ix"), lax.axis_size("ix")
    iy, ny = lax.axis_index("iy"), lax.axis_size("iy")
    me = lax.axis_index("depth")

    barrier = pltpu.get_barrier_semaphore()
    sides = (("ix", ix, nx), ("iy", iy, ny))

    half = layers // 2

    def swing(step):
        return jnp.where(lax.rem(step, 2) == 0, half + step // 2, half - (step + 1) // 2)

    def excused(front, behind):
        gap = behind - front
        return (gap > NEAR) & (gap < layers - NEAR)

    def greet(step, carry):
        other = lax.rem(me + swing(step), layers)

        @pl.when(jnp.logical_not(excused(other, me)))
        def _():
            pl.semaphore_signal(barrier, inc=1, device_id={"depth": other}, device_id_type=MESH)

        return carry

    def say(step, carry):
        other = lax.rem(me + swing(step), layers)

        @pl.when(excused(other, me))
        def _():
            pl.semaphore_signal(open_sem, inc=1, device_id={"depth": other}, device_id_type=MESH)

        return carry

    lax.fori_loop(0, layers - 1, greet, 0)
    for axis, place, size in sides:

        @pl.when(place > 0)
        def _():
            pl.semaphore_signal(barrier, inc=1, device_id={axis: place - 1}, device_id_type=MESH)

        @pl.when(place < size - 1)
        def _():
            pl.semaphore_signal(barrier, inc=1, device_id={axis: place + 1}, device_id_type=MESH)

    span = brick_y // CHUNKS

    def load(chunk):
        return pltpu.make_async_copy(
            density.at[:, pl.ds(chunk * span, span), :],
            brick.at[pl.ds(1, brick_z), pl.ds(ROWS + chunk * span, span), :],
            load_sem.at[chunk],
        )

    coeffs = [
        pltpu.make_async_copy(source, target, coeff_sem.at[number])
        for number, (source, target) in enumerate(
            ((opacity, opacity_s), (color, color_s), (light, light_s))
        )
    ]
    for copy in coeffs:
        copy.start()
    for chunk in range(CHUNKS):
        load(chunk).start()
    for copy in coeffs:
        copy.wait()
    root = math.sqrt(3.0 / (brick_z * layers) * math.log2(math.e))
    o0, o1, o2, o3 = (opacity_s[k] * (root / 4.0**k) for k in range(4))
    lx, ly, lz = (0.7 * light_s[k] for k in range(3))
    squares = []
    for channel in range(3):
        c0, c1, c2, c3 = (color_s[channel, k] for k in range(4))
        squares.append(
            [
                c0 * c0,
                2.0 * c0 * c1 / 4.0,
                (2.0 * c0 * c2 + c1 * c1) / 16.0,
                2.0 * (c0 * c3 + c1 * c2) / 64.0,
                (2.0 * c1 * c3 + c2 * c2) / 256.0,
                2.0 * c2 * c3 / 1024.0,
                c3 * c3 / 4096.0,
            ]
        )

    lane = lax.broadcasted_iota(jnp.int32, (ROWS, LANES), 1)
    even = lax.rem(lane, 2) == 0
    pair = lane // 2
    per_chunk = blocks // CHUNKS
    zero = jnp.zeros((ROWS, LANES), jnp.float32)

    def first_pass(chunk, carry):
        load(chunk).wait()
        base = pl.multiple_of(ROWS + chunk * span, ROWS)
        packed = [zero] * per_chunk
        for z in range(brick_z):
            here = pair == z
            for k in range(per_chunk):
                v = brick[z + 1, pl.ds(base + ROWS * k, ROWS), :]
                packed[k] = jnp.where(here, pltpu.roll(v, 2 * z + 1, 1), packed[k])
        first = pl.multiple_of(chunk * (span // 2), ROWS)
        for k in range(0, per_chunk, 2):
            a, b = packed[k], packed[k + 1]
            at = pl.ds(first + ROWS * (k // 2), ROWS)
            x_out[0, at, :] = jnp.where(even, pltpu.roll(a, LANES - 1, 1), b)
            x_out[1, at, :] = jnp.where(even, a, pltpu.roll(b, 1, 1))
        return carry

    def hide(block, carry):
        row = pl.multiple_of(ROWS * block, ROWS)
        total, clear = zero, zero + 1.0
        for z in range(brick_z):
            v = brick[z + 1, pl.ds(row + ROWS, ROWS), :]
            p = ((o3 * v + o2) * v + o1) * v + o0
            total = total - p * p
            after = jnp.exp2(total)
            opaque[z, pl.ds(row, ROWS), :] = clear - after
            clear = after
        sent_clear[block] = clear
        return carry

    lax.fori_loop(0, CHUNKS, first_pass, 0)
    y_out[0] = brick[pl.ds(1, brick_z), ROWS, :]
    y_out[1] = brick[pl.ds(1, brick_z), ROWS + brick_y - 1, :]

    def slopes(block, z):
        row = pl.multiple_of(ROWS * block, ROWS)
        gy = (
            brick[z + 1, pl.ds(row + ROWS + 1, ROWS), :]
            - brick[z + 1, pl.ds(row + ROWS - 1, ROWS), :]
        )
        gz = brick[z + 2, pl.ds(row + ROWS, ROWS), :] - brick[z, pl.ds(row + ROWS, ROWS), :]
        return gy * ly + gz * lz, gy * gy + (gz * gz + 4.0)

    def across(block, z):
        v = brick[z + 1, pl.ds(pl.multiple_of(ROWS * block + ROWS, ROWS), ROWS), :]
        return pltpu.roll(v, LANES - 1, 1) - pltpu.roll(v, 1, 1)

    def slope(block, carry=0):
        at = pl.ds(pl.multiple_of(ROWS * block, ROWS), ROWS)
        for z in range(1, brick_z - 1):
            dots[z, at, :], norms[z, at, :] = slopes(block, z)
            steps[z, at, :] = across(block, z)
        return carry

    early = jnp.where(me < half, blocks, jnp.clip(half * (me - half - NEAR), 0, blocks))
    lax.fori_loop(0, early, hide, 0)
    sloped = jnp.where(me < half - 2, blocks - 1, 1)
    lax.fori_loop(1, sloped, slope, 0)

    def plane(chunk):
        return pl.ds(ROWS + chunk * span, span)

    lanes = [
        (
            "depth",
            me,
            layers,
            (brick.at[1, plane(k), :], brick.at[brick_z + 1, plane(k), :]),
            (brick.at[brick_z, plane(k), :], brick.at[0, plane(k), :]),
        )
        for k in range(CHUNKS)
    ]
    lanes[1:1] = [
        ("ix", ix, nx, (x_out.at[0], x_in.at[1]), (x_out.at[1], x_in.at[0])),
        ("iy", iy, ny, (y_out.at[0], y_in.at[1]), (y_out.at[1], y_in.at[0])),
    ]
    halos = []
    for number, (axis, place, size, down, up) in enumerate(lanes):
        lower, upper = place > 0, place < size - 1
        for way, (go, come, (source, target), step) in enumerate(
            ((lower, upper, down, -1), (upper, lower, up, 1))
        ):
            copy = pltpu.make_async_remote_copy(
                src_ref=source,
                dst_ref=target,
                send_sem=halo_send.at[2 * number + way],
                recv_sem=halo_recv.at[2 * number + way],
                device_id={axis: place + step},
                device_id_type=MESH,
            )
            halos.append((copy, go, come, target))
    for _, _, come, target in halos:

        @pl.when(jnp.logical_not(come))
        def _():
            target[...] = jnp.zeros(target.shape, jnp.float32)

    some_excused = me <= layers - 2 - NEAR
    missing = jnp.clip(layers - 1 - NEAR - me, 0, layers - 1 - 2 * NEAR)
    greeted = layers - 1 - missing
    for _, place, size in sides:
        greeted = greeted + jnp.where(place > 0, 1, 0) + jnp.where(place < size - 1, 1, 0)
    pl.semaphore_wait(barrier, greeted)

    def leave(some):
        for copy, go, _, _ in some:

            @pl.when(go)
            def _():
                copy.start()

    leave(halos[:6])
    lax.fori_loop(early, blocks, hide, 0)
    leave(halos[6:])
    lax.fori_loop(0, layers - 1, say, 0)

    def clear_copy(block, layer):
        return pltpu.make_async_remote_copy(
            src_ref=sent_clear.at[block],
            dst_ref=clears.at[layer],
            send_sem=clear_send.at[block],
            recv_sem=clear_recv.at[layer],
            device_id={"depth": block},
            device_id_type=MESH,
        )

    def part_copy(block, layer):
        return pltpu.make_async_remote_copy(
            src_ref=sent.at[block],
            dst_ref=parts.at[layer],
            send_sem=part_send.at[block],
            recv_sem=part_recv.at[layer],
            device_id={"depth": block},
            device_id_type=MESH,
        )

    ahead = jnp.minimum(me, half // 2)
    second = jnp.clip(me - half // 2, 0, half // 2)

    behind_near = jnp.minimum(NEAR, layers - 1 - me)

    def centre(step):
        near = step - ahead
        front = near - behind_near
        return jnp.where(
            step < ahead,
            step,
            jnp.where(
                near < behind_near,
                me + behind_near - near,
                jnp.where(
                    front < me - ahead,
                    ahead + front,
                    jnp.where(front == me - ahead, me, layers - 1 - (step - me - behind_near - 1)),
                ),
            ),
        )

    def order(step):
        place = step - ahead
        later = place - jnp.where(place >= BETWEEN + second, second, 0)
        rest = half + lax.rem(later + me - half + 1, half)
        inside = (place >= BETWEEN) & (place < BETWEEN + second)
        usual = jnp.where(step < ahead, step, jnp.where(inside, half // 2 + place - BETWEEN, rest))
        return jnp.where(some_excused, centre(step), usual)

    def send_clear(step, carry):
        block = order(step)

        @pl.when((block != me) & jnp.logical_not(excused(me, block)))
        def _():
            clear_copy(block, me).start()

        return carry

    lax.fori_loop(0, blocks, send_clear, 0)

    def arrive(some):
        for copy, _, come, _ in some:

            @pl.when(come)
            def _():
                copy.wait_recv()

    lax.fori_loop(sloped, blocks - 1, slope, 0)
    arrive(halos[4:6])
    brick[pl.ds(1, brick_z), ROWS - 1, :] = y_in[0]
    brick[pl.ds(1, brick_z), ROWS + brick_y, :] = y_in[1]
    slope(0)
    slope(blocks - 1)
    arrive(halos[:4])

    def unpack(k, carry):
        at = pl.ds(pl.multiple_of(ROWS * k, ROWS), ROWS)
        last = x_in[1, at, :] - x_out[0, at, :]
        first = x_out[1, at, :] - x_in[0, at, :]
        row = pl.multiple_of(2 * ROWS * k, ROWS)
        x_halo[pl.ds(row, ROWS), :] = jnp.where(even, last, pltpu.roll(first, 1, 1))
        x_halo[pl.ds(row + ROWS, ROWS), :] = jnp.where(
            even, pltpu.roll(last, LANES - 1, 1), first
        )
        return carry

    lax.fori_loop(0, per_chunk // 2, unpack, 0)
    is_edge = (lane == 0) | (lane == LANES - 1)

    def shade(block):
        row = pl.multiple_of(ROWS * block, ROWS)
        at = pl.ds(row, ROWS)
        halo = x_halo[at, :]
        moments = [zero] * 7
        for z in range(brick_z):
            v = brick[z + 1, pl.ds(row + ROWS, ROWS), :]
            edge = pltpu.roll(halo, LANES - (2 * z + 1), 1)
            if z in (0, brick_z - 1):
                dot, norm = slopes(block, z)
                gx = across(block, z)
            else:
                dot, norm, gx = dots[z, at, :], norms[z, at, :], steps[z, at, :]
            gx = gx + jnp.where(is_edge, edge, 0.0)
            shading = jnp.abs(gx * lx + dot) * lax.rsqrt(gx * gx + norm) + 0.3
            weight = opaque[z, at, :] * shading
            moments[0] = moments[0] + weight
            for degree in range(1, 7):
                weight = weight * v
                moments[degree] = moments[degree] + weight
        for channel in range(3):
            q = squares[channel]
            value = q[0] * moments[0]
            for degree in range(1, 7):
                value = value + q[degree] * moments[degree]
            sent[block, channel] = value

    def each(step, carry):
        block = order(step)

        @pl.when(step == ahead)
        def _():
            arrive(halos[6:])
            lax.fori_loop(per_chunk // 2, blocks // 2, unpack, 0)

        shade(block)

        @pl.when((block != me) & jnp.logical_not(excused(me, block)))
        def _():
            part_copy(block, me).start()

        return carry

    lax.fori_loop(0, blocks - missing, each, 0)

    @pl.when(missing > 0)
    def _():
        pl.semaphore_wait(open_sem, missing)

    def each_excused(step, carry):
        block = order(step)
        clear_copy(block, me).start()
        shade(block)
        part_copy(block, me).start()
        return carry

    lax.fori_loop(blocks - missing, blocks, each_excused, 0)

    def finish(step, carry):
        block = lax.rem(me + step, layers)
        clear_copy(block, me).wait_send()
        part_copy(block, me).wait_send()
        return carry

    lax.fori_loop(1, layers, finish, 0)
    for copy, go, _, _ in halos:

        @pl.when(go)
        def _():
            copy.wait_send()

    clears[me] = sent_clear[me]
    parts[me] = sent[me]

    def gather(step, carry):
        layer = lax.rem(me + swing(layers - 2 - step), layers)
        clear_copy(layer, layer).wait_recv()
        part_copy(layer, layer).wait_recv()
        return carry

    lax.fori_loop(0, layers - 1, gather, 0)
    result, clear = [zero] * 3, zero + 1.0
    for layer in range(layers):
        result = [value + clear * parts[layer, k] for k, value in enumerate(result)]
        clear = clear * clears[layer]
    for channel, value in enumerate([*result, clear]):
        image[channel] = value


def per_device(*arguments):
    density = arguments[0]
    layers = lax.axis_size("depth")
    brick_z, brick_y, brick_x = density.shape
    blocks = brick_y // ROWS
    f32 = jnp.float32
    dma = pltpu.SemaphoreType.DMA
    return pl.pallas_call(
        functools.partial(kernel, layers),
        out_shape=jax.ShapeDtypeStruct((4, ROWS, brick_x), f32),
        in_specs=[pl.BlockSpec(memory_space=pltpu.HBM)] * 4,
        out_specs=pl.BlockSpec(memory_space=pltpu.VMEM),
        scratch_shapes=[
            pltpu.VMEM((brick_z + 2, brick_y + 2 * ROWS, brick_x), f32),
            *[pltpu.VMEM((brick_z, brick_y, brick_x), f32)] * 4,
            pltpu.VMEM((2, brick_y // 2, LANES), f32),
            pltpu.VMEM((2, brick_y // 2, LANES), f32),
            pltpu.VMEM((2, brick_z, LANES), f32),
            pltpu.VMEM((2, brick_z, LANES), f32),
            pltpu.VMEM((brick_y, LANES), f32),
            pltpu.VMEM((blocks, 3, ROWS, LANES), f32),
            pltpu.VMEM((layers, 3, ROWS, LANES), f32),
            pltpu.VMEM((blocks, ROWS, LANES), f32),
            pltpu.VMEM((layers, ROWS, LANES), f32),
            pltpu.SMEM((3, 4), f32),
            pltpu.SMEM((4,), f32),
            pltpu.SMEM((3,), f32),
            dma((CHUNKS,)),
            dma((3,)),
            dma((2 * CHUNKS + 4,)),
            dma((2 * CHUNKS + 4,)),
            dma((blocks,)),
            dma((layers,)),
            dma((blocks,)),
            dma((layers,)),
            pltpu.SemaphoreType.REGULAR,
        ],
        compiler_params=pltpu.CompilerParams(
            collective_id=0, has_side_effects=True, vmem_limit_bytes=32 << 20
        ),
    )(*(pltpu.with_memory_space_constraint(a, pltpu.HBM) for a in arguments))


def solution(mesh):
    return jax.shard_map(
        per_device,
        mesh=mesh,
        in_specs=(P("depth", "iy", "ix"), P(), P(), P()),
        out_specs=P(None, ("iy", "depth"), "ix"),
        check_vma=False,
    )
```

```python
import functools
import math

import jax
import jax.numpy as jnp
from jax import lax
from jax.experimental import pallas as pl
from jax.experimental.pallas import tpu as pltpu
from jax.sharding import PartitionSpec as P

MESH = pl.DeviceIdType.MESH
LANES = 128
ROWS = 8
CHUNKS = 4
BETWEEN = 2
NEAR = 4


def kernel(
    layers,
    density,
    color,
    opacity,
    light,
    image,
    brick,
    opaque,
    dots,
    norms,
    steps,
    x_out,
    x_in,
    y_out,
    y_in,
    x_halo,
    sent,
    parts,
    sent_clear,
    clears,
    color_s,
    opacity_s,
    light_s,
    load_sem,
    coeff_sem,
    halo_send,
    halo_recv,
    part_send,
    part_recv,
    clear_send,
    clear_recv,
    open_sem,
):
    brick_z, brick_y, _ = density.shape
    blocks = brick_y // ROWS
    ix, nx = lax.axis_index("ix"), lax.axis_size("ix")
    iy, ny = lax.axis_index("iy"), lax.axis_size("iy")
    me = lax.axis_index("depth")

    barrier = pltpu.get_barrier_semaphore()
    sides = (("ix", ix, nx), ("iy", iy, ny))

    half = layers // 2

    def swing(step):
        return jnp.where(lax.rem(step, 2) == 0, half + step // 2, half - (step + 1) // 2)

    def excused(front, behind):
        gap = behind - front
        return (gap > NEAR) & (gap < layers - NEAR)

    def greet(step, carry):
        other = lax.rem(me + swing(step), layers)

        @pl.when(jnp.logical_not(excused(other, me)))
        def _():
            pl.semaphore_signal(barrier, inc=1, device_id={"depth": other}, device_id_type=MESH)

        return carry

    def say(step, carry):
        other = lax.rem(me + swing(step), layers)

        @pl.when(excused(other, me))
        def _():
            pl.semaphore_signal(open_sem, inc=1, device_id={"depth": other}, device_id_type=MESH)

        return carry

    lax.fori_loop(0, layers - 1, greet, 0)
    for axis, place, size in sides:

        @pl.when(place > 0)
        def _():
            pl.semaphore_signal(barrier, inc=1, device_id={axis: place - 1}, device_id_type=MESH)

        @pl.when(place < size - 1)
        def _():
            pl.semaphore_signal(barrier, inc=1, device_id={axis: place + 1}, device_id_type=MESH)

    span = brick_y // CHUNKS

    def load(chunk):
        return pltpu.make_async_copy(
            density.at[:, pl.ds(chunk * span, span), :],
            brick.at[pl.ds(1, brick_z), pl.ds(ROWS + chunk * span, span), :],
            load_sem.at[chunk],
        )

    coeffs = [
        pltpu.make_async_copy(source, target, coeff_sem.at[number])
        for number, (source, target) in enumerate(
            ((opacity, opacity_s), (color, color_s), (light, light_s))
        )
    ]
    for copy in coeffs:
        copy.start()
    for chunk in range(CHUNKS):
        load(chunk).start()
    for copy in coeffs:
        copy.wait()
    root = math.sqrt(3.0 / (brick_z * layers) * math.log2(math.e))
    o0, o1, o2, o3 = (opacity_s[k] * (root / 4.0**k) for k in range(4))
    lx, ly, lz = (0.7 * light_s[k] for k in range(3))
    squares = []
    for channel in range(3):
        c0, c1, c2, c3 = (color_s[channel, k] for k in range(4))
        squares.append(
            [
                c0 * c0,
                2.0 * c0 * c1 / 4.0,
                (2.0 * c0 * c2 + c1 * c1) / 16.0,
                2.0 * (c0 * c3 + c1 * c2) / 64.0,
                (2.0 * c1 * c3 + c2 * c2) / 256.0,
                2.0 * c2 * c3 / 1024.0,
                c3 * c3 / 4096.0,
            ]
        )

    lane = lax.broadcasted_iota(jnp.int32, (ROWS, LANES), 1)
    even = lax.rem(lane, 2) == 0
    pair = lane // 2
    per_chunk = blocks // CHUNKS
    zero = jnp.zeros((ROWS, LANES), jnp.float32)

    def first_pass(chunk, carry):
        load(chunk).wait()
        base = pl.multiple_of(ROWS + chunk * span, ROWS)
        packed = [zero] * per_chunk
        for z in range(brick_z):
            here = pair == z
            for k in range(per_chunk):
                v = brick[z + 1, pl.ds(base + ROWS * k, ROWS), :]
                packed[k] = jnp.where(here, pltpu.roll(v, 2 * z + 1, 1), packed[k])
        first = pl.multiple_of(chunk * (span // 2), ROWS)
        for k in range(0, per_chunk, 2):
            a, b = packed[k], packed[k + 1]
            at = pl.ds(first + ROWS * (k // 2), ROWS)
            x_out[0, at, :] = jnp.where(even, pltpu.roll(a, LANES - 1, 1), b)
            x_out[1, at, :] = jnp.where(even, a, pltpu.roll(b, 1, 1))
        return carry

    def hide(block, carry):
        row = pl.multiple_of(ROWS * block, ROWS)
        total, clear = zero, zero + 1.0
        for z in range(brick_z):
            v = brick[z + 1, pl.ds(row + ROWS, ROWS), :]
            p = ((o3 * v + o2) * v + o1) * v + o0
            total = total - p * p
            after = jnp.exp2(total)
            opaque[z, pl.ds(row, ROWS), :] = clear - after
            clear = after
        sent_clear[block] = clear
        return carry

    lax.fori_loop(0, CHUNKS, first_pass, 0)
    y_out[0] = brick[pl.ds(1, brick_z), ROWS, :]
    y_out[1] = brick[pl.ds(1, brick_z), ROWS + brick_y - 1, :]

    def slopes(block, z):
        row = pl.multiple_of(ROWS * block, ROWS)
        gy = (
            brick[z + 1, pl.ds(row + ROWS + 1, ROWS), :]
            - brick[z + 1, pl.ds(row + ROWS - 1, ROWS), :]
        )
        gz = brick[z + 2, pl.ds(row + ROWS, ROWS), :] - brick[z, pl.ds(row + ROWS, ROWS), :]
        return gy * ly + gz * lz, gy * gy + (gz * gz + 4.0)

    def across(block, z):
        v = brick[z + 1, pl.ds(pl.multiple_of(ROWS * block + ROWS, ROWS), ROWS), :]
        return pltpu.roll(v, LANES - 1, 1) - pltpu.roll(v, 1, 1)

    def slope(block, carry=0):
        at = pl.ds(pl.multiple_of(ROWS * block, ROWS), ROWS)
        for z in range(1, brick_z - 1):
            dots[z, at, :], norms[z, at, :] = slopes(block, z)
            steps[z, at, :] = across(block, z)
        return carry

    early = jnp.where(me < half, blocks, jnp.clip(half * (me - half - NEAR), 0, blocks))
    lax.fori_loop(0, early, hide, 0)
    sloped = jnp.where(me < half - 2, blocks - 1, 1)
    lax.fori_loop(1, sloped, slope, 0)

    def plane(chunk):
        return pl.ds(ROWS + chunk * span, span)

    lanes = [
        (
            "depth",
            me,
            layers,
            (brick.at[1, plane(k), :], brick.at[brick_z + 1, plane(k), :]),
            (brick.at[brick_z, plane(k), :], brick.at[0, plane(k), :]),
        )
        for k in range(CHUNKS)
    ]
    lanes[1:1] = [
        ("ix", ix, nx, (x_out.at[0], x_in.at[1]), (x_out.at[1], x_in.at[0])),
        ("iy", iy, ny, (y_out.at[0], y_in.at[1]), (y_out.at[1], y_in.at[0])),
    ]
    halos = []
    for number, (axis, place, size, down, up) in enumerate(lanes):
        lower, upper = place > 0, place < size - 1
        for way, (go, come, (source, target), step) in enumerate(
            ((lower, upper, down, -1), (upper, lower, up, 1))
        ):
            copy = pltpu.make_async_remote_copy(
                src_ref=source,
                dst_ref=target,
                send_sem=halo_send.at[2 * number + way],
                recv_sem=halo_recv.at[2 * number + way],
                device_id={axis: place + step},
                device_id_type=MESH,
            )
            halos.append((copy, go, come, target))
    for _, _, come, target in halos:

        @pl.when(jnp.logical_not(come))
        def _():
            target[...] = jnp.zeros(target.shape, jnp.float32)

    some_excused = me <= layers - 2 - NEAR
    missing = jnp.clip(layers - 1 - NEAR - me, 0, layers - 1 - 2 * NEAR)
    greeted = layers - 1 - missing
    for _, place, size in sides:
        greeted = greeted + jnp.where(place > 0, 1, 0) + jnp.where(place < size - 1, 1, 0)
    pl.semaphore_wait(barrier, greeted)

    def leave(some):
        for copy, go, _, _ in some:

            @pl.when(go)
            def _():
                copy.start()

    leave(halos[:6])
    lax.fori_loop(early, blocks, hide, 0)
    leave(halos[6:])
    lax.fori_loop(0, layers - 1, say, 0)

    def clear_copy(block, layer):
        return pltpu.make_async_remote_copy(
            src_ref=sent_clear.at[block],
            dst_ref=clears.at[layer],
            send_sem=clear_send.at[block],
            recv_sem=clear_recv.at[layer],
            device_id={"depth": block},
            device_id_type=MESH,
        )

    def part_copy(block, layer):
        return pltpu.make_async_remote_copy(
            src_ref=sent.at[block],
            dst_ref=parts.at[layer],
            send_sem=part_send.at[block],
            recv_sem=part_recv.at[layer],
            device_id={"depth": block},
            device_id_type=MESH,
        )

    ahead = jnp.minimum(me, half // 2)
    second = jnp.clip(me - half // 2, 0, half // 2)

    behind_near = jnp.minimum(NEAR, layers - 1 - me)

    def centre(step):
        near = step - ahead
        front = near - behind_near
        return jnp.where(
            step < ahead,
            step,
            jnp.where(
                near < behind_near,
                me + behind_near - near,
                jnp.where(
                    front < me - ahead,
                    ahead + front,
                    jnp.where(front == me - ahead, me, layers - 1 - (step - me - behind_near - 1)),
                ),
            ),
        )

    yields = (me >= half // 2) & (lax.rem(iy, 2) == 1)

    def order(step):
        held = yields & (step >= 2) & (step < 6)
        step = jnp.where(held, 2 + lax.rem(step, 4), step)
        place = step - ahead
        later = place - jnp.where(place >= BETWEEN + second, second, 0)
        rest = half + lax.rem(later + me - half + 1, half)
        inside = (place >= BETWEEN) & (place < BETWEEN + second)
        usual = jnp.where(step < ahead, step, jnp.where(inside, half // 2 + place - BETWEEN, rest))
        return jnp.where(some_excused, centre(step), usual)

    def send_clear(step, carry):
        block = order(step)

        @pl.when((block != me) & jnp.logical_not(excused(me, block)))
        def _():
            clear_copy(block, me).start()

        return carry

    lax.fori_loop(0, blocks, send_clear, 0)

    def arrive(some):
        for copy, _, come, _ in some:

            @pl.when(come)
            def _():
                copy.wait_recv()

    lax.fori_loop(sloped, blocks - 1, slope, 0)
    arrive(halos[4:6])
    brick[pl.ds(1, brick_z), ROWS - 1, :] = y_in[0]
    brick[pl.ds(1, brick_z), ROWS + brick_y, :] = y_in[1]
    slope(0)
    slope(blocks - 1)
    arrive(halos[:4])

    def unpack(k, carry):
        at = pl.ds(pl.multiple_of(ROWS * k, ROWS), ROWS)
        last = x_in[1, at, :] - x_out[0, at, :]
        first = x_out[1, at, :] - x_in[0, at, :]
        row = pl.multiple_of(2 * ROWS * k, ROWS)
        x_halo[pl.ds(row, ROWS), :] = jnp.where(even, last, pltpu.roll(first, 1, 1))
        x_halo[pl.ds(row + ROWS, ROWS), :] = jnp.where(
            even, pltpu.roll(last, LANES - 1, 1), first
        )
        return carry

    lax.fori_loop(0, per_chunk // 2, unpack, 0)
    is_edge = (lane == 0) | (lane == LANES - 1)

    def shade(block):
        row = pl.multiple_of(ROWS * block, ROWS)
        at = pl.ds(row, ROWS)
        halo = x_halo[at, :]
        moments = [zero] * 7
        for z in range(brick_z):
            v = brick[z + 1, pl.ds(row + ROWS, ROWS), :]
            edge = pltpu.roll(halo, LANES - (2 * z + 1), 1)
            if z in (0, brick_z - 1):
                dot, norm = slopes(block, z)
                gx = across(block, z)
            else:
                dot, norm, gx = dots[z, at, :], norms[z, at, :], steps[z, at, :]
            gx = gx + jnp.where(is_edge, edge, 0.0)
            shading = jnp.abs(gx * lx + dot) * lax.rsqrt(gx * gx + norm) + 0.3
            weight = opaque[z, at, :] * shading
            moments[0] = moments[0] + weight
            for degree in range(1, 7):
                weight = weight * v
                moments[degree] = moments[degree] + weight
        for channel in range(3):
            q = squares[channel]
            value = q[0] * moments[0]
            for degree in range(1, 7):
                value = value + q[degree] * moments[degree]
            sent[block, channel] = value

    def each(step, carry):
        block = order(step)

        @pl.when(step == jnp.where(yields, 2, ahead))
        def _():
            arrive(halos[6:])
            lax.fori_loop(per_chunk // 2, blocks // 2, unpack, 0)

        shade(block)

        @pl.when((block != me) & jnp.logical_not(excused(me, block)))
        def _():
            part_copy(block, me).start()

        return carry

    lax.fori_loop(0, blocks - missing, each, 0)

    @pl.when(missing > 0)
    def _():
        pl.semaphore_wait(open_sem, missing)

    def each_excused(step, carry):
        block = order(step)
        clear_copy(block, me).start()
        shade(block)
        part_copy(block, me).start()
        return carry

    lax.fori_loop(blocks - missing, blocks, each_excused, 0)

    def finish(step, carry):
        block = lax.rem(me + step, layers)
        clear_copy(block, me).wait_send()
        part_copy(block, me).wait_send()
        return carry

    lax.fori_loop(1, layers, finish, 0)
    for copy, go, _, _ in halos:

        @pl.when(go)
        def _():
            copy.wait_send()

    clears[me] = sent_clear[me]
    parts[me] = sent[me]

    def gather(step, carry):
        layer = lax.rem(me + swing(layers - 2 - step), layers)
        clear_copy(layer, layer).wait_recv()
        part_copy(layer, layer).wait_recv()
        return carry

    lax.fori_loop(0, layers - 1, gather, 0)
    result, clear = [zero] * 3, zero + 1.0
    for layer in range(layers):
        result = [value + clear * parts[layer, k] for k, value in enumerate(result)]
        clear = clear * clears[layer]
    for channel, value in enumerate([*result, clear]):
        image[channel] = value


def per_device(*arguments):
    density = arguments[0]
    layers = lax.axis_size("depth")
    brick_z, brick_y, brick_x = density.shape
    blocks = brick_y // ROWS
    f32 = jnp.float32
    dma = pltpu.SemaphoreType.DMA
    return pl.pallas_call(
        functools.partial(kernel, layers),
        out_shape=jax.ShapeDtypeStruct((4, ROWS, brick_x), f32),
        in_specs=[pl.BlockSpec(memory_space=pltpu.HBM)] * 4,
        out_specs=pl.BlockSpec(memory_space=pltpu.VMEM),
        scratch_shapes=[
            pltpu.VMEM((brick_z + 2, brick_y + 2 * ROWS, brick_x), f32),
            *[pltpu.VMEM((brick_z, brick_y, brick_x), f32)] * 4,
            pltpu.VMEM((2, brick_y // 2, LANES), f32),
            pltpu.VMEM((2, brick_y // 2, LANES), f32),
            pltpu.VMEM((2, brick_z, LANES), f32),
            pltpu.VMEM((2, brick_z, LANES), f32),
            pltpu.VMEM((brick_y, LANES), f32),
            pltpu.VMEM((blocks, 3, ROWS, LANES), f32),
            pltpu.VMEM((layers, 3, ROWS, LANES), f32),
            pltpu.VMEM((blocks, ROWS, LANES), f32),
            pltpu.VMEM((layers, ROWS, LANES), f32),
            pltpu.SMEM((3, 4), f32),
            pltpu.SMEM((4,), f32),
            pltpu.SMEM((3,), f32),
            dma((CHUNKS,)),
            dma((3,)),
            dma((2 * CHUNKS + 4,)),
            dma((2 * CHUNKS + 4,)),
            dma((blocks,)),
            dma((layers,)),
            dma((blocks,)),
            dma((layers,)),
            pltpu.SemaphoreType.REGULAR,
        ],
        compiler_params=pltpu.CompilerParams(
            collective_id=0, has_side_effects=True, vmem_limit_bytes=32 << 20
        ),
    )(*(pltpu.with_memory_space_constraint(a, pltpu.HBM) for a in arguments))


def solution(mesh):
    return jax.shard_map(
        per_device,
        mesh=mesh,
        in_specs=(P("depth", "iy", "ix"), P(), P(), P()),
        out_specs=P(None, ("iy", "depth"), "ix"),
        check_vma=False,
    )
```
